256 devices in a mesh: blk: 32 (over x_hi, z, core), col: 8 (over x_lo, y).
Axes of the slice: x: 4 (x_hi: 2, x_lo: 2; x = x_hi * 2 + x_lo), y: 4, z: 8, core: 2. Of those that a mesh axis runs over, the one named last changes fastest.
Arguments:
- amplitudes: bfloat16 [1024, 32768], P('blk', 'col'), may hold values from -6 to 6
- integrals: bfloat16 [32768, 32768], P('blk', 'col'), may hold values from -0.03125 to 0.03125
- amp_mask: int32 [1024, 256], P('blk', 'col'), may hold values 0 or 1
- int_mask: int32 [256, 256], P('blk', 'col'), may hold values 0 or 1
Outputs:
- ladder: bfloat16 [1024, 32768], P('col', 'blk')
The draws below stay inside these ranges and needn't reach their ends.
All inputs are finite; a program needn't handle non-finite values. No bound on the sum of `amp_mask` or of `int_mask` on one device may be relied on, other than what follows from the above.
Results may differ from the reference program's by a relative error of at most 0.001.
Values may be sent and summed in bfloat16 or wider, within the bound.
No kernel may reach another device: no remote copies, remote signals or barrier semaphores. Data moves between devices by JAX's collectives and lax.ppermute only.
A program may use at most 64 MiB of HBM per device.

```python
import jax
import jax.numpy as jnp
from jax import lax

TILE = 128
RT = 8
NT = 256
P_SIZE = 32768
OPAIRS = 1024
N_BLK = 32


def with_ends(drawn, stream_key, smallest, high):
    spot = [jax.random.randint(jax.random.fold_in(stream_key, axis), (), 0, length) for axis, length in enumerate(drawn.shape)]
    widest = drawn.shape.index(max(drawn.shape))
    next_to = spot[:widest] + [(spot[widest] + 1) % drawn.shape[widest]] + spot[widest + 1:]
    return drawn.at[tuple(spot)].set(smallest).at[tuple(next_to)].set(high)


def block_levels(key, dims, pieces, least, largest):
    factor_of, own = 1.0, jax.random.fold_in(key, 6)
    for dim, blocks in pieces:
        heights = jnp.exp(jax.random.uniform(jax.random.fold_in(own, dim), (blocks,), jnp.float32, least / len(pieces), largest / len(pieces)))
        factor_of = factor_of * jnp.repeat(heights, dims[dim] // blocks).reshape([-1 if axis == dim else 1 for axis in range(len(dims))])
    return factor_of


def bell_draw(own_key, shape, width, limit, shards=(), dtype=jnp.bfloat16):
    result = width * jax.random.normal(own_key, shape, jnp.float32)
    if shards:
        result = result * block_levels(own_key, shape, shards, -0.22, 0.18)
    return jnp.clip(result, -limit, limit).astype(dtype)


def setup_inputs(seed: int = 0) -> dict:
    streams_of = jax.random.split(jax.random.key(seed), 5)
    return {
        "amplitudes": bell_draw(streams_of[0], (OPAIRS, P_SIZE), 1.0, 6.0, ((0, 32), (1, 8))),
        "integrals": bell_draw(streams_of[1], (P_SIZE, P_SIZE), P_SIZE ** -0.5, 0.03125, ((0, 32), (1, 8))),
        "amp_mask": with_ends((jax.random.randint(streams_of[2], (OPAIRS, NT), 0, 2) < 1).astype(jnp.int32), jax.random.fold_in(streams_of[2], 1), 0, 1),
        "int_mask": with_ends((jax.random.randint(streams_of[3], (NT, NT), 0, 2) < 1).astype(jnp.int32), jax.random.fold_in(streams_of[3], 1), 0, 1),
    }


def reference(amplitudes, integrals, amp_mask, int_mask):
    kept_amps = (amplitudes.reshape(OPAIRS, NT, TILE) * amp_mask.astype(jnp.bfloat16)[:, :, None]).reshape(OPAIRS, P_SIZE)
    row_blocks = integrals.reshape(N_BLK, RT * TILE, P_SIZE)
    mask_blocks = int_mask.reshape(N_BLK, RT, NT)

    def one_block(inputs):
        block, block_mask = inputs
        kept = (block.reshape(RT, TILE, NT, TILE) * block_mask.astype(jnp.bfloat16)[:, None, :, None]).reshape(RT * TILE, P_SIZE)
        return lax.dot_general(kept_amps, kept, (((1,), (1,)), ((), ())), preferred_element_type=jnp.float32)

    results = lax.map(one_block, (row_blocks, mask_blocks))
    return results.transpose(1, 0, 2).reshape(OPAIRS, P_SIZE).astype(jnp.bfloat16)
```

```python
import jax
import jax.numpy as jnp
from jax import lax
from jax.experimental import pallas as pl
from jax.experimental.pallas import tpu as pltpu
from jax.sharding import Mesh, PartitionSpec as P

TILE = 128
OWN = 32
TILES = 32
GROUP = 8
WIN = 256
LOW = (0, 80, 240, 320)
ROWS = 576
MSG = ROWS + OWN
F32 = jnp.float32
BF16 = jnp.bfloat16


def swap(x, axis):
    return lax.ppermute(x, axis, [(0, 1), (1, 0)])


def pack_kernel(amps_ref, mask_ref, msg_ref, kept_ref, over_ref, acc):
    mask = mask_ref[...].astype(F32)
    row = lax.broadcasted_iota(jnp.int32, (OWN, OWN), 0)
    col = lax.broadcasted_iota(jnp.int32, (OWN, OWN), 1)
    below = (col < row).astype(BF16)
    mask16 = mask.astype(BF16)
    in_tile = jnp.dot(below, mask16, preferred_element_type=F32)
    count = jnp.dot(jnp.ones((OWN, OWN), BF16), mask16, preferred_element_type=F32)
    same = row // GROUP == col // GROUP
    before = jnp.dot(count.astype(BF16), ((row < col) & same).astype(BF16), preferred_element_type=F32)
    in_group = in_tile + before
    lane = lax.broadcasted_iota(jnp.int32, (OWN, TILES), 1) // GROUP
    total = [
        jnp.sum(jnp.where(lane == g, count, 0.0), axis=1, keepdims=True) for g in range(4)
    ]
    start1 = jnp.maximum(total[0], float(LOW[1]))
    end1 = start1 + total[1]
    start3 = ROWS - total[3]
    start2 = jnp.minimum(start3, float(LOW[2] + WIN)) - total[2]
    over = (end1 > LOW[1] + WIN) | (start2 < LOW[2]) | (end1 > start2)
    over_ref[...] = jnp.broadcast_to(jnp.where(over, 1, 0)[:8], (8, TILE)).astype(jnp.int32)
    offset = jnp.where(
        lane == 0,
        0.0,
        jnp.where(lane == 1, start1 - LOW[1], jnp.where(lane == 2, start2 - LOW[2], start3 - LOW[3])),
    )
    place = jnp.where(mask > 0.0, in_group + offset, -1.0)
    msg_ref[ROWS:MSG, :] = jnp.concatenate([place, jnp.zeros((OWN, TILE - TILES), F32)], axis=1).astype(BF16)
    acc[...] = jnp.zeros_like(acc)
    spots = lax.broadcasted_iota(jnp.int32, (OWN, WIN), 1).astype(F32)
    for g in range(4):
        hot, val = [], []
        for t in range(g * GROUP, (g + 1) * GROUP):
            tile = amps_ref[:, t * TILE : (t + 1) * TILE]
            kept_ref[:, t * TILE : (t + 1) * TILE] = tile * mask16[:, t : t + 1]
            hot.append((place[:, t : t + 1] == spots).astype(BF16))
            val.append(tile)
        hot = jnp.concatenate(hot, axis=0)
        val = jnp.concatenate(val, axis=0)
        acc[LOW[g] : LOW[g] + WIN, :] += lax.dot_general(
            hot, val, (((0,), (0,)), ((), ())), preferred_element_type=F32
        )
    msg_ref[:ROWS, :] = acc[...].astype(BF16)


def pack(amps, mask):
    return pl.pallas_call(
        pack_kernel,
        out_shape=(
            jax.ShapeDtypeStruct((MSG, TILE), BF16),
            jax.ShapeDtypeStruct(amps.shape, BF16),
            jax.ShapeDtypeStruct((8, TILE), jnp.int32),
        ),
        scratch_shapes=[pltpu.VMEM((ROWS, TILE), F32)],
        compiler_params=pltpu.CompilerParams(vmem_limit_bytes=16 << 20),
    )(amps, mask)


def unpack_kernel(core_ref, own_ref, other_ref, out_ref):
    core = core_ref[0]
    spots = lax.broadcasted_iota(jnp.int32, (OWN, WIN), 1).astype(F32)
    for ref, which in ((own_ref, core), (other_ref, 1 - core)):
        rows = pl.ds(pl.multiple_of(which * OWN, OWN), OWN)
        place = ref[0, ROWS:MSG, :].astype(F32)
        for g in range(4):
            hot = jnp.concatenate(
                [(place[:, t : t + 1] == spots).astype(BF16) for t in range(g * GROUP, (g + 1) * GROUP)],
                axis=0,
            )
            got = jnp.dot(hot, ref[0, LOW[g] : LOW[g] + WIN, :], preferred_element_type=F32).astype(BF16)
            for i in range(GROUP):
                t = g * GROUP + i
                out_ref[rows, t * TILE : (t + 1) * TILE] = got[i * OWN : (i + 1) * OWN, :]


def unpack(core, own, other):
    n = own.shape[0]
    return pl.pallas_call(
        unpack_kernel,
        grid=(n,),
        in_specs=[
            pl.BlockSpec(memory_space=pltpu.SMEM),
            pl.BlockSpec((1, MSG, TILE), lambda i: (i, 0, 0)),
            pl.BlockSpec((1, MSG, TILE), lambda i: (i, 0, 0)),
        ],
        out_specs=pl.BlockSpec((2 * OWN, TILES * TILE), lambda i: (i, 0)),
        out_shape=jax.ShapeDtypeStruct((n * 2 * OWN, TILES * TILE), BF16),
        compiler_params=pltpu.CompilerParams(vmem_limit_bytes=16 << 20),
        cost_estimate=pl.CostEstimate(flops=4_000_000_000, bytes_accessed=6 << 20, transcendentals=0),
    )(core, own, other)


def local(amplitudes, integrals, amp_mask, int_mask):
    row_count, col_count = integrals.shape
    msg, kept_amps, over = pack(amplitudes, amp_mask)

    far = swap(msg, "xh")
    gathered = [lax.all_gather(m, "z", axis=0) for m in (msg, far)]

    for axis, size in (("z", 8), ("y", 4)):
        hop = 1
        while hop < size:
            over = jnp.maximum(over, lax.ppermute(over, axis, [(i, (i + hop) % size) for i in range(size)]))
            hop *= 2
    for axis in ("core", "xh", "xl"):
        over = jnp.maximum(over, swap(over, axis))
    full = over[0, 0] > 0

    kept_ints = (
        integrals.reshape(row_count // TILE, TILE, col_count // TILE, TILE)
        * int_mask.astype(BF16)[:, None, :, None]
    ).reshape(row_count, col_count)
    kept_ints = lax.optimization_barrier(kept_ints)

    core = lax.axis_index("core").reshape(1)
    sums = []
    for chunk in range(2):
        own = gathered[chunk]
        other = swap(own, "core")

        def slow(kept, own, other):
            kept = kept if chunk == 0 else swap(kept, "xh")
            return lax.all_gather(kept, ("z", "core"), axis=0, tiled=True)

        amps = lax.cond(full, slow, lambda kept, own, other: unpack(core, own, other), kept_amps, own, other)
        partial_value = lax.dot_general(amps, kept_ints, (((1,), (1,)), ((), ())), preferred_element_type=F32)
        parts = lax.all_to_all(partial_value.reshape(4, -1, row_count), "y", 0, 0)
        sums.append(jnp.sum(parts, axis=0))
    near = lax.axis_index("xl") == lax.axis_index("xh")
    mine = jnp.where(near, sums[0], sums[1])
    sent = jnp.where(near, sums[1], sums[0])
    return (mine + swap(sent, "xl")).astype(BF16)


def solution(mesh):
    fine = Mesh(mesh.devices.reshape(2, 8, 2, 2, 4), ("xh", "z", "core", "xl", "y"))
    blk, col = ("xh", "z", "core"), ("xl", "y")
    return jax.shard_map(
        local, mesh=fine, in_specs=(P(blk, col),) * 4, out_specs=P(col, blk), check_vma=False
    )
```

```python
import jax
import jax.numpy as jnp
from jax import lax
from jax.experimental import pallas as pl
from jax.experimental.pallas import tpu as pltpu
from jax.sharding import Mesh, PartitionSpec as P

TILE = 128
OWN = 32
TILES = 32
GROUP = 8
WIN = 256
LOW = (0, 80, 240, 320)
ROWS = 576
MSG = ROWS + OWN
RT = 8
BIG = 32000.0
F32 = jnp.float32
BF16 = jnp.bfloat16
I16 = jnp.int16
I32 = jnp.int32
VMEM = pl.BlockSpec(memory_space=pltpu.VMEM)
SMEM = pl.BlockSpec(memory_space=pltpu.SMEM)


def swap(x, axis):
    return lax.ppermute(x, axis, [(0, 1), (1, 0)])


def pack_kernel(amps_ref, mask_ref, msg_ref, acc):
    mask = mask_ref[...].astype(F32)
    row = lax.broadcasted_iota(I32, (OWN, OWN), 0)
    col = lax.broadcasted_iota(I32, (OWN, OWN), 1)
    mask16 = mask.astype(BF16)
    in_tile = jnp.dot((col < row).astype(BF16), mask16, preferred_element_type=F32)
    count = jnp.dot(jnp.ones((OWN, OWN), BF16), mask16, preferred_element_type=F32)
    same = row // GROUP == col // GROUP
    before = jnp.dot(count.astype(BF16), ((row < col) & same).astype(BF16), preferred_element_type=F32)
    lane = col // GROUP
    total = [jnp.sum(jnp.where(lane == g, count, 0.0), axis=1, keepdims=True) for g in range(4)]
    start1 = jnp.maximum(total[0], float(LOW[1]))
    end1 = start1 + total[1]
    start3 = ROWS - total[3]
    start2 = jnp.minimum(start3, float(LOW[2] + WIN)) - total[2]
    over = (end1 > LOW[1] + WIN) | (start2 < LOW[2]) | (end1 > start2)
    offset = jnp.where(
        lane == 0,
        0.0,
        jnp.where(lane == 1, start1 - LOW[1], jnp.where(lane == 2, start2 - LOW[2], start3 - LOW[3])),
    )
    place = jnp.where(mask > 0.0, in_tile + before + offset, -1.0)
    over = jnp.broadcast_to(jnp.where(over, 1.0, 0.0), (OWN, TILE - TILES))
    msg_ref[0, ROWS:MSG, :] = jnp.concatenate([place, over], axis=1).astype(BF16)
    acc[...] = jnp.zeros_like(acc)
    spots = lax.broadcasted_iota(I32, (OWN, WIN), 1).astype(F32)
    for g in range(4):
        tiles = range(g * GROUP, (g + 1) * GROUP)
        hot = jnp.concatenate([(place[:, t : t + 1] == spots).astype(BF16) for t in tiles], axis=0)
        val = jnp.concatenate([amps_ref[:, t * TILE : (t + 1) * TILE] for t in tiles], axis=0)
        acc[LOW[g] : LOW[g] + WIN, :] += lax.dot_general(
            hot, val, (((0,), (0,)), ((), ())), preferred_element_type=F32
        )
    msg_ref[0, :ROWS, :] = acc[...].astype(BF16)


def pack(amps, mask):
    return pl.pallas_call(
        pack_kernel,
        out_shape=jax.ShapeDtypeStruct((1, MSG, TILE), BF16),
        scratch_shapes=[pltpu.VMEM((ROWS, TILE), F32)],
        compiler_params=pltpu.CompilerParams(vmem_limit_bytes=8 << 20),
    )(amps, mask)


def keep_kernel(mask_ref, ints_ref, out_ref):
    r = pl.program_id(0)
    for t in range(TILES):
        kept = jnp.where(mask_ref[r, t] > 0, 1.0, 0.0).astype(BF16)
        out_ref[:, t * TILE : (t + 1) * TILE] = ints_ref[:, t * TILE : (t + 1) * TILE] * kept


def keep(ints, mask):
    block = pl.BlockSpec((TILE, TILES * TILE), lambda r: (r, 0))
    return pl.pallas_call(
        keep_kernel,
        grid=(RT,),
        in_specs=[SMEM, block],
        out_specs=block,
        out_shape=jax.ShapeDtypeStruct(ints.shape, BF16),
        compiler_params=pltpu.CompilerParams(vmem_limit_bytes=8 << 20),
        cost_estimate=pl.CostEstimate(flops=4 << 20, bytes_accessed=16 << 20, transcendentals=0),
    )(mask, ints)


def unpack_kernel(sizes, row_ref, *refs):
    ins, (out_ref, over_ref, buf, top) = refs[: len(sizes)], refs[len(sizes) :]
    i = pl.program_id(0)
    low = 0
    for size, ref in zip(sizes, ins, strict=True):

        @pl.when((i >= low) & (i < low + size))
        def _(ref=ref, low=low):
            buf[...] = ref[i - low]

        low += size
    place = buf[ROWS:MSG, :].astype(F32)
    seen = jnp.where(i == 0, 0.0, top[...])
    top[...] = jnp.maximum(seen, place[:8, :])
    over_ref[...] = jnp.broadcast_to(top[:, TILE - 1 :], (8, TILE)).astype(I32)
    spots = lax.broadcasted_iota(I32, (OWN, WIN), 1).astype(F32)
    for g in range(4):
        tiles = range(g * GROUP, (g + 1) * GROUP)
        hot = jnp.concatenate([(place[:, t : t + 1] == spots).astype(BF16) for t in tiles], axis=0)
        got = jnp.dot(hot, buf[LOW[g] : LOW[g] + WIN, :], preferred_element_type=F32).astype(BF16)
        for n, t in enumerate(tiles):
            out_ref[:, t * TILE : (t + 1) * TILE] = got[n * OWN : (n + 1) * OWN, :]


def unpack(rows, messages):
    sizes = [m.shape[0] for m in messages]
    whole = [pl.BlockSpec(m.shape, lambda i, rows: (0, 0, 0)) for m in messages]
    return pl.pallas_call(
        lambda *refs: unpack_kernel(sizes, *refs),
        grid_spec=pltpu.PrefetchScalarGridSpec(
            num_scalar_prefetch=1,
            grid=(sum(sizes),),
            in_specs=whole,
            out_specs=[
                pl.BlockSpec((OWN, TILES * TILE), lambda i, rows: (rows[i], 0)),
                pl.BlockSpec((8, TILE), lambda i, rows: (0, 0)),
            ],
            scratch_shapes=[pltpu.VMEM((MSG, TILE), BF16), pltpu.VMEM((8, TILE), F32)],
        ),
        out_shape=[
            jax.ShapeDtypeStruct((sum(sizes) * OWN, TILES * TILE), BF16),
            jax.ShapeDtypeStruct((8, TILE), I32),
        ],
        compiler_params=pltpu.CompilerParams(vmem_limit_bytes=16 << 20),
        cost_estimate=pl.CostEstimate(flops=5_000_000_000, bytes_accessed=7 << 20, transcendentals=0),
    )(rows, *messages)


def code(value):
    most = jnp.max(jnp.abs(value), axis=1, keepdims=True)
    power = jnp.ceil(jnp.log2(jnp.maximum(most, 1e-37)))
    return jnp.round(value * jnp.exp2(-power) * BIG).astype(I32).astype(I16), power


def decode(msg_ref, t):
    scale = jnp.exp2(msg_ref[RT, :, t : t + 1].astype(I32).astype(F32))
    return msg_ref[t].astype(I32).astype(F32) * (1.0 / BIG) * scale


def product_kernel(amps_ref, over_ref, ints_ref, own_ref, *outs):
    j = pl.program_id(0)
    value = lax.dot_general(amps_ref[...], ints_ref[...], (((1,), (1,)), ((), ())), preferred_element_type=F32)
    lane = lax.broadcasted_iota(I32, (TILE, TILE), 1)
    for n in range(2):
        t = 2 * j + n
        own_ref[t] = value[:TILE, n * TILE : (n + 1) * TILE]
        for d, out in enumerate(outs):
            coded, power = code(value[(d + 1) * TILE : (d + 2) * TILE, n * TILE : (n + 1) * TILE])
            out[t] = coded
            flag = jnp.broadcast_to(over_ref[:1, :], (TILE, TILE))
            before = jnp.where(t == 0, flag, out[RT].astype(I32))
            out[RT] = jnp.where(lane == t, power.astype(I32), before).astype(I16)


def product(amps, over, ints):
    coded = jax.ShapeDtypeStruct((RT + 1, TILE, TILE), I16)
    whole = lambda shape: pl.BlockSpec(shape, lambda j: (0,) * len(shape))
    return pl.pallas_call(
        product_kernel,
        grid=(RT // 2,),
        in_specs=[
            whole(amps.shape),
            whole(over.shape),
            pl.BlockSpec((2 * TILE, TILES * TILE), lambda j: (j, 0)),
        ],
        out_specs=[whole((RT, TILE, TILE))] + [whole(coded.shape)] * 3,
        out_shape=[jax.ShapeDtypeStruct((RT, TILE, TILE), F32)] + [coded] * 3,
        compiler_params=pltpu.CompilerParams(vmem_limit_bytes=32 << 20),
        cost_estimate=pl.CostEstimate(flops=6_000_000_000, bytes_accessed=16 << 20, transcendentals=0),
    )(amps, over, ints)


def add_kernel(over_ref, own_ref, a_ref, b_ref, c_ref, sum_ref, out_ref):
    lane = lax.broadcasted_iota(I32, (TILE, TILE), 1)
    powers = jnp.broadcast_to(over_ref[:1, :], (TILE, TILE))
    for ref in (a_ref, b_ref, c_ref):
        powers = jnp.maximum(powers, ref[RT].astype(I32))
    for t in range(RT):
        value = own_ref[t] + decode(a_ref, t) + decode(b_ref, t) + decode(c_ref, t)
        sum_ref[t] = value
        out_ref[t], power = code(value)
        powers = jnp.where(lane == t, power.astype(I32), powers)
    out_ref[RT] = powers.astype(I16)


def add(over, own, parts):
    return pl.pallas_call(
        add_kernel,
        in_specs=[VMEM] * 5,
        out_specs=[VMEM] * 2,
        out_shape=[
            jax.ShapeDtypeStruct(own.shape, F32),
            jax.ShapeDtypeStruct((RT + 1, TILE, TILE), I16),
        ],
        compiler_params=pltpu.CompilerParams(vmem_limit_bytes=8 << 20),
    )(over, own, *parts)


def last_kernel(near_ref, first_ref, second_ref, flag_ref, got_ref, out_ref, over_ref):
    near = near_ref[0] > 0
    for t in range(RT):
        mine = jnp.where(near, first_ref[t], second_ref[t])
        out_ref[:, t * TILE : (t + 1) * TILE] = (mine + decode(got_ref, t)).astype(BF16)
    over_ref[...] = jnp.maximum(
        got_ref[RT, :16, TILE - 16 :].astype(I32), flag_ref[RT, :16, TILE - 16 :].astype(I32)
    )


def last(near, first, second, flag, got):
    return pl.pallas_call(
        last_kernel,
        in_specs=[SMEM] + [VMEM] * 4,
        out_specs=[VMEM] * 2,
        out_shape=[jax.ShapeDtypeStruct((TILE, RT * TILE), BF16), jax.ShapeDtypeStruct((16, 16), I32)],
        compiler_params=pltpu.CompilerParams(vmem_limit_bytes=8 << 20),
    )(near, first, second, flag, got)


def plain(amplitudes, amp_mask, kept_ints):
    kept = (
        amplitudes.reshape(OWN, TILES, TILE) * amp_mask.astype(BF16)[:, :, None]
    ).reshape(OWN, TILES * TILE)
    value = lax.dot_general(
        lax.all_gather(kept, ("xh", "z", "core"), axis=0, tiled=True),
        kept_ints,
        (((1,), (1,)), ((), ())),
        preferred_element_type=F32,
    )
    return lax.psum_scatter(value, ("xl", "y"), scatter_dimension=0, tiled=True).astype(BF16)


RING = [(2 * z, 2 * ((z + 1) % 8)) for z in range(8)] + [(2 * z + 1, 2 * ((z + 7) % 8) + 1) for z in range(8)]

SHIFT = (0, 0, -1, -1, 1, 1, -2, -2, 2, 2, -3, -3, 3, 3, 4, 4)
OTHER = (0, 1, 0, 1, 1, 0, 0, 1, 1, 0, 0, 1, 1, 0, 0, 1)


def local(amplitudes, integrals, amp_mask, int_mask):
    z, core, y = (lax.axis_index(name).astype(I32) for name in ("z", "core", "y"))
    near = lax.axis_index("xl") == lax.axis_index("xh")
    up = 1 - 2 * core

    own = pack(amplitudes, amp_mask)
    pair = jnp.concatenate([own, swap(own, "core")], axis=0)
    pairs = [pair, swap(pair, "xh")]
    kept_ints = keep(integrals, int_mask)

    far = (z + up * jnp.asarray(SHIFT, I32)) & 7
    rows = (((far >> 1) - y) & 3) * 4 + (far & 1) * 2 + (core ^ jnp.asarray(OTHER, I32))

    held = [[pair] for pair in pairs]
    for hop in range(1, 5):
        for chunk in range(2):
            block = held[chunk][-2] if hop > 1 else held[chunk][0]
            block = lax.ppermute(block if hop < 4 else block[:1], ("z", "core"), RING)
            held[chunk] += [block, swap(block, "core")]

    sums, coded = [], []
    over = None
    for chunk in range(2):
        amps, flag = unpack(rows, held[chunk])
        over = flag if over is None else jnp.maximum(over, flag)
        own_part, *parts = product(amps, over, kept_ints)
        got = [
            lax.ppermute(part, "y", [(i, (i + d + 1) % 4) for i in range(4)]) for d, part in enumerate(parts)
        ]
        total, sent = add(over, own_part, got)
        sums.append(total)
        coded.append(sent)
    sent = jnp.where(near, coded[1], coded[0])
    sent = sent.at[RT, :, TILE - 16 :].set(coded[1][RT, :, TILE - 16 :])
    got = swap(sent, "xl")
    out, over = last(near.astype(I32).reshape(1), sums[0], sums[1], sent, got)
    return lax.cond(
        jnp.max(over) > 0,
        lambda out: plain(amplitudes, amp_mask, kept_ints),
        lambda out: out,
        out,
    )


def solution(mesh):
    fine = Mesh(mesh.devices.reshape(2, 8, 2, 2, 4), ("xh", "z", "core", "xl", "y"))
    blk, col = ("xh", "z", "core"), ("xl", "y")
    return jax.shard_map(
        local, mesh=fine, in_specs=(P(blk, col),) * 4, out_specs=P(col, blk), check_vma=False
    )
```

```python
import jax
import jax.numpy as jnp
from jax import lax
from jax.experimental import pallas as pl
from jax.experimental.pallas import tpu as pltpu
from jax.sharding import Mesh, PartitionSpec as P

TILE = 128
OWN = 32
TILES = 32
GROUP = 8
WIN = 256
LOW = (0, 80, 240, 320)
ROWS = 576
MSG = ROWS + OWN
RT = 8
META = 16
BIG = 32000.0
F32 = jnp.float32
BF16 = jnp.bfloat16
I16 = jnp.int16
I32 = jnp.int32
VMEM = pl.BlockSpec(memory_space=pltpu.VMEM)
SMEM = pl.BlockSpec(memory_space=pltpu.SMEM)


def swap(x, axis):
    return lax.ppermute(x, axis, [(0, 1), (1, 0)])


def pack_kernel(amps_ref, mask_ref, msg_ref, acc):
    mask = mask_ref[...].astype(F32)
    row = lax.broadcasted_iota(I32, (OWN, OWN), 0)
    col = lax.broadcasted_iota(I32, (OWN, OWN), 1)
    mask16 = mask.astype(BF16)
    in_tile = jnp.dot((col < row).astype(BF16), mask16, preferred_element_type=F32)
    count = jnp.dot(jnp.ones((OWN, OWN), BF16), mask16, preferred_element_type=F32)
    same = row // GROUP == col // GROUP
    before = jnp.dot(count.astype(BF16), ((row < col) & same).astype(BF16), preferred_element_type=F32)
    lane = col // GROUP
    total = [jnp.sum(jnp.where(lane == g, count, 0.0), axis=1, keepdims=True) for g in range(4)]
    start1 = jnp.maximum(total[0], float(LOW[1]))
    end1 = start1 + total[1]
    start3 = ROWS - total[3]
    start2 = jnp.minimum(start3, float(LOW[2] + WIN)) - total[2]
    over = (end1 > LOW[1] + WIN) | (start2 < LOW[2]) | (end1 > start2)
    offset = jnp.where(
        lane == 0,
        0.0,
        jnp.where(lane == 1, start1 - LOW[1], jnp.where(lane == 2, start2 - LOW[2], start3 - LOW[3])),
    )
    place = jnp.where(mask > 0.0, in_tile + before + offset, -1.0)
    over = jnp.broadcast_to(jnp.where(over, 1.0, 0.0), (OWN, TILE - TILES))
    msg_ref[0, ROWS:MSG, :] = jnp.concatenate([place, over], axis=1).astype(BF16)
    acc[...] = jnp.zeros_like(acc)
    spots = lax.broadcasted_iota(I32, (OWN, WIN), 1).astype(F32)
    for g in range(4):
        tiles = range(g * GROUP, (g + 1) * GROUP)
        hot = jnp.concatenate([(place[:, t : t + 1] == spots).astype(BF16) for t in tiles], axis=0)
        val = jnp.concatenate([amps_ref[:, t * TILE : (t + 1) * TILE] for t in tiles], axis=0)
        acc[LOW[g] : LOW[g] + WIN, :] += lax.dot_general(
            hot, val, (((0,), (0,)), ((), ())), preferred_element_type=F32
        )
    msg_ref[0, :ROWS, :] = acc[...].astype(BF16)


def pack(amps, mask):
    return pl.pallas_call(
        pack_kernel,
        out_shape=jax.ShapeDtypeStruct((1, MSG, TILE), BF16),
        scratch_shapes=[pltpu.VMEM((ROWS, TILE), F32)],
        compiler_params=pltpu.CompilerParams(vmem_limit_bytes=8 << 20),
    )(amps, mask)


def code(value):
    most = jnp.max(jnp.abs(value), axis=1, keepdims=True)
    power = jnp.ceil(jnp.log2(jnp.maximum(most, 1e-37)))
    return jnp.round(value * jnp.exp2(-power) * BIG).astype(I32).astype(I16), power


def tile_rows(t):
    return pl.ds(t * TILE, TILE)


def scales(msg_ref):
    powers = msg_ref[RT * TILE :, :].astype(I32).astype(F32)
    return jnp.exp2(jnp.transpose(jnp.concatenate([powers] * (TILE // META), axis=0)))


def decode(msg_ref, scale, t):
    return msg_ref[tile_rows(t), :].astype(I32).astype(F32) * (1.0 / BIG) * scale[:, t : t + 1]


def flags(msg_ref):
    return msg_ref[RT * TILE :, :].astype(I32)


def powers_and_flags(powers, flag):
    row = lax.broadcasted_iota(I32, (META, TILE), 0)
    powers = jnp.transpose(powers)[:META, :].astype(I32)
    return jnp.where(row < RT, powers, flag).astype(I16)


def chunk_kernel(sizes, row_ref, mask_ref, before_ref, ints_ref, *refs):
    ins, (own_ref, a_ref, b_ref, c_ref, over_ref, got, amps, held, sem) = refs[: len(sizes)], refs[len(sizes) :]
    loads = [
        pltpu.make_async_copy(ints_ref.at[pl.ds(j * 2 * TILE, 2 * TILE), :], held.at[j], sem.at[j])
        for j in range(RT // 2)
    ]
    for load in loads:
        load.start()
    i = 0
    for size, ref in zip(sizes, ins, strict=True):
        got[i : i + size] = ref[...]
        i += size
    spots = lax.broadcasted_iota(I32, (OWN, WIN), 1).astype(F32)

    def unpack(i, over):
        place = got[i, ROWS:MSG, :].astype(F32)
        rows = pl.ds(pl.multiple_of(row_ref[i] * OWN, OWN), OWN)
        for g in range(4):
            tiles = range(g * GROUP, (g + 1) * GROUP)
            hot = jnp.concatenate([(place[:, t : t + 1] == spots).astype(BF16) for t in tiles], axis=0)
            value = jnp.dot(hot, got[i, LOW[g] : LOW[g] + WIN, :], preferred_element_type=F32).astype(BF16)
            for n, t in enumerate(tiles):
                amps[rows, t * TILE : (t + 1) * TILE] = value[n * OWN : (n + 1) * OWN, :]
        return jnp.maximum(over, place[:META, TILE - 1 :])

    over = lax.fori_loop(0, i, unpack, jnp.zeros((META, 1), F32))
    over = jnp.maximum(jnp.broadcast_to(over, (META, TILE)).astype(I32), before_ref[...])
    over_ref[...] = over
    lane = lax.broadcasted_iota(I32, (TILE, TILE), 1)
    for load in loads:
        load.wait()

    def multiply(j, powers):
        for n in range(2):
            for t in range(TILES):
                kept = jnp.where(mask_ref[2 * j + n, t] > 0, 1.0, 0.0).astype(BF16)
                part = (j, slice(n * TILE, (n + 1) * TILE), slice(t * TILE, (t + 1) * TILE))
                held[part] = held[part] * kept
        value = lax.dot_general(amps[...], held[j], (((1,), (1,)), ((), ())), preferred_element_type=F32)
        for n in range(2):
            t = 2 * j + n
            own_ref[t] = value[:TILE, n * TILE : (n + 1) * TILE]
            new = []
            for d, out in enumerate((a_ref, b_ref, c_ref)):
                coded, power = code(value[(d + 1) * TILE : (d + 2) * TILE, n * TILE : (n + 1) * TILE])
                out[pl.ds(pl.multiple_of(t * TILE, TILE), TILE), :] = coded
                new.append(jnp.where(lane == t, power, powers[d]))
            powers = tuple(new)
        return powers

    powers = lax.fori_loop(0, RT // 2, multiply, (jnp.zeros((TILE, TILE), F32),) * 3)
    for d, out in enumerate((a_ref, b_ref, c_ref)):
        out[RT * TILE :, :] = powers_and_flags(powers[d], over)


def chunk_sums(rows, mask, before, ints, messages):
    sizes = [m.shape[0] for m in messages]
    coded = jax.ShapeDtypeStruct((RT * TILE + META, TILE), I16)
    return pl.pallas_call(
        lambda *refs: chunk_kernel(sizes, *refs),
        in_specs=[SMEM, SMEM, VMEM, pl.BlockSpec(memory_space=pl.ANY)] + [VMEM] * len(sizes),
        out_specs=[VMEM] * 5,
        out_shape=[
            jax.ShapeDtypeStruct((RT, TILE, TILE), F32),
            coded,
            coded,
            coded,
            jax.ShapeDtypeStruct((META, TILE), I32),
        ],
        scratch_shapes=[
            pltpu.VMEM((sum(sizes), MSG, TILE), BF16),
            pltpu.VMEM((sum(sizes) * OWN, TILES * TILE), BF16),
            pltpu.VMEM((RT // 2, 2 * TILE, TILES * TILE), BF16),
            pltpu.SemaphoreType.DMA((RT // 2,)),
        ],
        compiler_params=pltpu.CompilerParams(vmem_limit_bytes=44 << 20),
        cost_estimate=pl.CostEstimate(flops=10_000_000_000, bytes_accessed=16 << 20, transcendentals=0),
    )(rows, mask, before, ints, *messages)


def add_kernel(over_ref, own_ref, a_ref, b_ref, c_ref, sum_ref, out_ref):
    lane = lax.broadcasted_iota(I32, (TILE, TILE), 1)
    parts = (a_ref, b_ref, c_ref)
    scale = [scales(ref) for ref in parts]
    powers = jnp.zeros((TILE, TILE), F32)
    for t in range(RT):
        value = own_ref[t]
        for ref, by in zip(parts, scale, strict=True):
            value = value + decode(ref, by, t)
        sum_ref[t] = value
        out_ref[tile_rows(t), :], power = code(value)
        powers = jnp.where(lane == t, power, powers)
    flag = over_ref[...]
    for ref in parts:
        flag = jnp.maximum(flag, jnp.broadcast_to(flags(ref)[META - 1 :, :], (META, TILE)))
    out_ref[RT * TILE :, :] = powers_and_flags(powers, flag)


def add(over, own, parts):
    return pl.pallas_call(
        add_kernel,
        in_specs=[VMEM] * 5,
        out_specs=[VMEM] * 2,
        out_shape=[
            jax.ShapeDtypeStruct(own.shape, F32),
            jax.ShapeDtypeStruct((RT * TILE + META, TILE), I16),
        ],
        compiler_params=pltpu.CompilerParams(vmem_limit_bytes=8 << 20),
    )(over, own, *parts)


def choose_kernel(near_ref, first_ref, second_ref, out_ref):
    near = near_ref[0] > 0
    both = RT * TILE
    out_ref[:both, :] = jnp.where(near, second_ref[:both, :].astype(I32), first_ref[:both, :].astype(I32)).astype(I16)
    first, second = flags(first_ref), flags(second_ref)
    row = lax.broadcasted_iota(I32, (META, TILE), 0)
    out_ref[both:, :] = jnp.where((row >= RT) | near, second, first).astype(I16)


def choose(near, first, second):
    return pl.pallas_call(
        choose_kernel,
        in_specs=[SMEM] + [VMEM] * 2,
        out_specs=VMEM,
        out_shape=jax.ShapeDtypeStruct(first.shape, I16),
        compiler_params=pltpu.CompilerParams(vmem_limit_bytes=8 << 20),
    )(near, first, second)


def last_kernel(near_ref, first_ref, second_ref, sent_ref, got_ref, out_ref, over_ref):
    near = near_ref[0] > 0
    scale = scales(got_ref)
    for t in range(RT):
        mine = jnp.where(near, first_ref[t], second_ref[t])
        out_ref[:, t * TILE : (t + 1) * TILE] = (mine + decode(got_ref, scale, t)).astype(BF16)
    over_ref[...] = jnp.maximum(flags(sent_ref), flags(got_ref))


def last(near, first, second, sent, got):
    return pl.pallas_call(
        last_kernel,
        in_specs=[SMEM] + [VMEM] * 4,
        out_specs=[VMEM] * 2,
        out_shape=[jax.ShapeDtypeStruct((TILE, RT * TILE), BF16), jax.ShapeDtypeStruct((META, TILE), I32)],
        compiler_params=pltpu.CompilerParams(vmem_limit_bytes=8 << 20),
    )(near, first, second, sent, got)


def plain(amplitudes, integrals, amp_mask, int_mask):
    kept = (
        amplitudes.reshape(OWN, TILES, TILE) * amp_mask.astype(BF16)[:, :, None]
    ).reshape(OWN, TILES * TILE)
    copies = jnp.broadcast_to(kept, (32,) + kept.shape)
    every = lax.all_to_all(copies, ("xh", "z", "core"), 0, 0).reshape(32 * OWN, TILES * TILE)
    ints = (
        integrals.reshape(RT, TILE, TILES, TILE) * int_mask.astype(BF16)[:, None, :, None]
    ).reshape(integrals.shape)
    value = lax.dot_general(every, ints, (((1,), (1,)), ((), ())), preferred_element_type=F32)
    parts = lax.all_to_all(value.reshape(8, TILE, RT * TILE), ("xl", "y"), 0, 0)
    return jnp.sum(parts, axis=0).astype(BF16)


RING = [(2 * z, 2 * ((z + 1) % 8)) for z in range(8)] + [(2 * z + 1, 2 * ((z + 7) % 8) + 1) for z in range(8)]

SHIFT = (0, 0, -1, -1, 1, 1, -2, -2, 2, 2, -3, -3, 3, 3, 4, 4)
OTHER = (0, 1, 0, 1, 1, 0, 0, 1, 1, 0, 0, 1, 1, 0, 0, 1)


def local(amplitudes, integrals, amp_mask, int_mask):
    z, core, y = (lax.axis_index(name).astype(I32) for name in ("z", "core", "y"))
    near = lax.axis_index("xl") == lax.axis_index("xh")
    up = 1 - 2 * core

    far = (z + up * jnp.asarray(SHIFT, I32)) & 7
    rows = (((far >> 1) - y) & 3) * 4 + (far & 1) * 2 + (core ^ jnp.asarray(OTHER, I32))

    own = pack(amplitudes, amp_mask)
    block = jnp.concatenate([own, swap(own, "core")], axis=0)
    held = [[block], [swap(block, "xh")]]
    for hop in range(1, 5):
        block = lax.ppermute(block if hop < 4 else block[:1], ("z", "core"), RING)
        other = swap(block, "xh")
        held[0] += [block, swap(block, "core")]
        held[1] += [other, swap(other, "core")]

    sums, coded = [], []
    over = jnp.zeros((META, TILE), I32)
    for chunk in range(2):
        own_part, *parts, over = chunk_sums(rows, int_mask, over, integrals, held[chunk])
        got = [
            lax.ppermute(part, "y", [(i, (i + d + 1) % 4) for i in range(4)]) for d, part in enumerate(parts)
        ]
        total, sent = add(over, own_part, got)
        sums.append(total)
        coded.append(sent)
    near = near.astype(I32).reshape(1)
    sent = choose(near, *coded)
    out, over = last(near, *sums, sent, swap(sent, "xl"))
    return lax.cond(
        jnp.max(over[META - 1]) > 0,
        lambda out: plain(amplitudes, integrals, amp_mask, int_mask),
        lambda out: out,
        out,
    )


def solution(mesh):
    fine = Mesh(mesh.devices.reshape(2, 8, 2, 2, 4), ("xh", "z", "core", "xl", "y"))
    blk, col = ("xh", "z", "core"), ("xl", "y")
    return jax.shard_map(
        local, mesh=fine, in_specs=(P(blk, col),) * 4, out_specs=P(col, blk), check_vma=False
    )
```

```python
import jax
import jax.numpy as jnp
from jax import lax
from jax.experimental import pallas as pl
from jax.experimental.pallas import tpu as pltpu
from jax.sharding import Mesh, PartitionSpec as P

TILE = 128
OWN = 32
TILES = 32
GROUP = 8
WIN = 256
LOW = (0, 80, 240, 320)
ROWS = 576
MSG = ROWS + OWN
RT = 8
META = 16
BIG = 32000.0
F32 = jnp.float32
BF16 = jnp.bfloat16
I16 = jnp.int16
I32 = jnp.int32
VMEM = pl.BlockSpec(memory_space=pltpu.VMEM)
SMEM = pl.BlockSpec(memory_space=pltpu.SMEM)


def swap(x, axis):
    return lax.ppermute(x, axis, [(0, 1), (1, 0)])


def pack_kernel(amps_ref, mask_ref, msg_ref, acc):
    mask = mask_ref[...].astype(F32)
    row = lax.broadcasted_iota(I32, (OWN, OWN), 0)
    col = lax.broadcasted_iota(I32, (OWN, OWN), 1)
    mask16 = mask.astype(BF16)
    in_tile = jnp.dot((col < row).astype(BF16), mask16, preferred_element_type=F32)
    count = jnp.dot(jnp.ones((OWN, OWN), BF16), mask16, preferred_element_type=F32)
    same = row // GROUP == col // GROUP
    before = jnp.dot(count.astype(BF16), ((row < col) & same).astype(BF16), preferred_element_type=F32)
    lane = col // GROUP
    total = [jnp.sum(jnp.where(lane == g, count, 0.0), axis=1, keepdims=True) for g in range(4)]
    start1 = jnp.maximum(total[0], float(LOW[1]))
    end1 = start1 + total[1]
    start3 = ROWS - total[3]
    start2 = jnp.minimum(start3, float(LOW[2] + WIN)) - total[2]
    over = (end1 > LOW[1] + WIN) | (start2 < LOW[2]) | (end1 > start2)
    offset = jnp.where(
        lane == 0,
        0.0,
        jnp.where(lane == 1, start1 - LOW[1], jnp.where(lane == 2, start2 - LOW[2], start3 - LOW[3])),
    )
    place = jnp.where(mask > 0.0, in_tile + before + offset, -1.0)
    over = jnp.broadcast_to(jnp.where(over, 1.0, 0.0), (OWN, TILE - TILES))
    msg_ref[0, ROWS:MSG, :] = jnp.concatenate([place, over], axis=1).astype(BF16)
    acc[...] = jnp.zeros_like(acc)
    spots = lax.broadcasted_iota(I32, (OWN, WIN), 1).astype(F32)
    for g in range(4):
        tiles = range(g * GROUP, (g + 1) * GROUP)
        hot = jnp.concatenate([(place[:, t : t + 1] == spots).astype(BF16) for t in tiles], axis=0)
        val = jnp.concatenate([amps_ref[:, t * TILE : (t + 1) * TILE] for t in tiles], axis=0)
        acc[LOW[g] : LOW[g] + WIN, :] += lax.dot_general(
            hot, val, (((0,), (0,)), ((), ())), preferred_element_type=F32
        )
    msg_ref[0, :ROWS, :] = acc[...].astype(BF16)


def pack(amps, mask):
    return pl.pallas_call(
        pack_kernel,
        out_shape=jax.ShapeDtypeStruct((1, MSG, TILE), BF16),
        scratch_shapes=[pltpu.VMEM((ROWS, TILE), F32)],
        compiler_params=pltpu.CompilerParams(vmem_limit_bytes=8 << 20),
    )(amps, mask)


def code(value):
    most = jnp.max(jnp.abs(value), axis=1, keepdims=True)
    power = jnp.ceil(jnp.log2(jnp.maximum(most, 1e-37)))
    return jnp.round(value * jnp.exp2(-power) * BIG).astype(I32).astype(I16), power


def tile_rows(t):
    return pl.ds(t * TILE, TILE)


def scales(msg_ref):
    powers = msg_ref[RT * TILE :, :].astype(I32).astype(F32)
    return jnp.exp2(jnp.transpose(jnp.concatenate([powers] * (TILE // META), axis=0)))


def decode(msg_ref, scale, t):
    return msg_ref[tile_rows(t), :].astype(I32).astype(F32) * (1.0 / BIG) * scale[:, t : t + 1]


def flags(msg_ref):
    return msg_ref[RT * TILE :, :].astype(I32)


def powers_and_flags(powers, flag):
    row = lax.broadcasted_iota(I32, (META, TILE), 0)
    powers = jnp.transpose(powers)[:META, :].astype(I32)
    return jnp.where(row < RT, powers, flag).astype(I16)


def chunk_kernel(sizes, mask, row_ref, *refs):
    if mask:
        mask_ref, *refs = refs
    before_ref, ints_ref, *refs = refs
    ins, refs = refs[: len(sizes)], refs[len(sizes) :]
    own_ref, a_ref, b_ref, c_ref, over_ref, *refs = refs
    if mask:
        kept_ref, *refs = refs
    got, amps, held, sem = refs
    blocks = [pl.ds(j * 2 * TILE, 2 * TILE) for j in range(RT // 2)]
    loads = [pltpu.make_async_copy(ints_ref.at[rows, :], held.at[j], sem.at[0, j]) for j, rows in enumerate(blocks)]
    for load in loads:
        load.start()
    i = 0
    for size, ref in zip(sizes, ins, strict=True):
        got[i : i + size] = ref[...]
        i += size
    spots = lax.broadcasted_iota(I32, (OWN, WIN), 1).astype(F32)

    def unpack(i, over):
        place = got[i, ROWS:MSG, :].astype(F32)
        rows = pl.ds(pl.multiple_of(row_ref[i] * OWN, OWN), OWN)
        for g in range(4):
            tiles = range(g * GROUP, (g + 1) * GROUP)
            hot = jnp.concatenate([(place[:, t : t + 1] == spots).astype(BF16) for t in tiles], axis=0)
            value = jnp.dot(hot, got[i, LOW[g] : LOW[g] + WIN, :], preferred_element_type=F32).astype(BF16)
            for n, t in enumerate(tiles):
                amps[rows, t * TILE : (t + 1) * TILE] = value[n * OWN : (n + 1) * OWN, :]
        return jnp.maximum(over, place[:META, TILE - 1 :])

    over = lax.fori_loop(0, i, unpack, jnp.zeros((META, 1), F32), unroll=4)
    over = jnp.maximum(jnp.broadcast_to(over, (META, TILE)).astype(I32), before_ref[...])
    over_ref[...] = over
    lane = lax.broadcasted_iota(I32, (TILE, TILE), 1)
    powers = [jnp.zeros((TILE, TILE), F32)] * 3
    stores = []
    for j, load in enumerate(loads):
        load.wait()
        if mask:
            for n in range(2):
                for t in range(TILES):
                    kept = jnp.where(mask_ref[2 * j + n, t] > 0, 1.0, 0.0).astype(BF16)
                    part = (j, slice(n * TILE, (n + 1) * TILE), slice(t * TILE, (t + 1) * TILE))
                    held[part] = held[part] * kept
            stores.append(pltpu.make_async_copy(held.at[j], kept_ref.at[blocks[j], :], sem.at[1, j]))
            stores[j].start()
        value = lax.dot_general(amps[...], held[j], (((1,), (1,)), ((), ())), preferred_element_type=F32)
        for n in range(2):
            t = 2 * j + n
            own_ref[t] = value[:TILE, n * TILE : (n + 1) * TILE]
            for d, out in enumerate((a_ref, b_ref, c_ref)):
                coded, power = code(value[(d + 1) * TILE : (d + 2) * TILE, n * TILE : (n + 1) * TILE])
                out[t * TILE : (t + 1) * TILE, :] = coded
                powers[d] = jnp.where(lane == t, power, powers[d])
    for d, out in enumerate((a_ref, b_ref, c_ref)):
        out[RT * TILE :, :] = powers_and_flags(powers[d], over)
    for store in stores:
        store.wait()


def chunk_sums(rows, before, ints, messages, mask=None):
    sizes = [m.shape[0] for m in messages]
    masks = [] if mask is None else [mask]
    coded = jax.ShapeDtypeStruct((RT * TILE + META, TILE), I16)
    anywhere = pl.BlockSpec(memory_space=pl.ANY)
    return pl.pallas_call(
        lambda *refs: chunk_kernel(sizes, mask is not None, *refs),
        in_specs=[SMEM] * (1 + len(masks)) + [VMEM, anywhere] + [VMEM] * len(sizes),
        out_specs=[VMEM] * 5 + [anywhere] * len(masks),
        out_shape=[
            jax.ShapeDtypeStruct((RT, TILE, TILE), F32),
            coded,
            coded,
            coded,
            jax.ShapeDtypeStruct((META, TILE), I32),
        ]
        + [jax.ShapeDtypeStruct(ints.shape, BF16)] * len(masks),
        scratch_shapes=[
            pltpu.VMEM((sum(sizes), MSG, TILE), BF16),
            pltpu.VMEM((sum(sizes) * OWN, TILES * TILE), BF16),
            pltpu.VMEM((RT // 2, 2 * TILE, TILES * TILE), BF16),
            pltpu.SemaphoreType.DMA((2, RT // 2)),
        ],
        compiler_params=pltpu.CompilerParams(vmem_limit_bytes=44 << 20),
        cost_estimate=pl.CostEstimate(flops=10_000_000_000, bytes_accessed=16 << 20, transcendentals=0),
    )(rows, *masks, before, ints, *messages)


def add_kernel(over_ref, own_ref, a_ref, b_ref, c_ref, sum_ref, out_ref):
    lane = lax.broadcasted_iota(I32, (TILE, TILE), 1)
    parts = (a_ref, b_ref, c_ref)
    scale = [scales(ref) for ref in parts]
    powers = jnp.zeros((TILE, TILE), F32)
    for t in range(RT):
        value = own_ref[t]
        for ref, by in zip(parts, scale, strict=True):
            value = value + decode(ref, by, t)
        sum_ref[t] = value
        out_ref[tile_rows(t), :], power = code(value)
        powers = jnp.where(lane == t, power, powers)
    flag = over_ref[...]
    for ref in parts:
        flag = jnp.maximum(flag, jnp.broadcast_to(flags(ref)[META - 1 :, :], (META, TILE)))
    out_ref[RT * TILE :, :] = powers_and_flags(powers, flag)


def add(over, own, parts):
    return pl.pallas_call(
        add_kernel,
        in_specs=[VMEM] * 5,
        out_specs=[VMEM] * 2,
        out_shape=[
            jax.ShapeDtypeStruct(own.shape, F32),
            jax.ShapeDtypeStruct((RT * TILE + META, TILE), I16),
        ],
        compiler_params=pltpu.CompilerParams(vmem_limit_bytes=8 << 20),
    )(over, own, *parts)


def choose_kernel(near_ref, first_ref, second_ref, out_ref):
    near = near_ref[0] > 0
    both = RT * TILE
    out_ref[:both, :] = jnp.where(near, second_ref[:both, :].astype(I32), first_ref[:both, :].astype(I32)).astype(I16)
    first, second = flags(first_ref), flags(second_ref)
    row = lax.broadcasted_iota(I32, (META, TILE), 0)
    out_ref[both:, :] = jnp.where((row >= RT) | near, second, first).astype(I16)


def choose(near, first, second):
    return pl.pallas_call(
        choose_kernel,
        in_specs=[SMEM] + [VMEM] * 2,
        out_specs=VMEM,
        out_shape=jax.ShapeDtypeStruct(first.shape, I16),
        compiler_params=pltpu.CompilerParams(vmem_limit_bytes=8 << 20),
    )(near, first, second)


def last_kernel(near_ref, first_ref, second_ref, sent_ref, got_ref, out_ref, over_ref):
    near = near_ref[0] > 0
    scale = scales(got_ref)
    for t in range(RT):
        mine = jnp.where(near, first_ref[t], second_ref[t])
        out_ref[:, t * TILE : (t + 1) * TILE] = (mine + decode(got_ref, scale, t)).astype(BF16)
    over_ref[...] = jnp.maximum(flags(sent_ref), flags(got_ref))


def last(near, first, second, sent, got):
    return pl.pallas_call(
        last_kernel,
        in_specs=[SMEM] + [VMEM] * 4,
        out_specs=[VMEM] * 2,
        out_shape=[jax.ShapeDtypeStruct((TILE, RT * TILE), BF16), jax.ShapeDtypeStruct((META, TILE), I32)],
        compiler_params=pltpu.CompilerParams(vmem_limit_bytes=8 << 20),
    )(near, first, second, sent, got)


def plain(amplitudes, integrals, amp_mask, int_mask):
    kept = (
        amplitudes.reshape(OWN, TILES, TILE) * amp_mask.astype(BF16)[:, :, None]
    ).reshape(OWN, TILES * TILE)
    copies = jnp.broadcast_to(kept, (32,) + kept.shape)
    every = lax.all_to_all(copies, ("xh", "z", "core"), 0, 0).reshape(32 * OWN, TILES * TILE)
    ints = (
        integrals.reshape(RT, TILE, TILES, TILE) * int_mask.astype(BF16)[:, None, :, None]
    ).reshape(integrals.shape)
    value = lax.dot_general(every, ints, (((1,), (1,)), ((), ())), preferred_element_type=F32)
    parts = lax.all_to_all(value.reshape(8, TILE, RT * TILE), ("xl", "y"), 0, 0)
    return jnp.sum(parts, axis=0).astype(BF16)


RING = [(2 * z, 2 * ((z + 1) % 8)) for z in range(8)] + [(2 * z + 1, 2 * ((z + 7) % 8) + 1) for z in range(8)]

SHIFT = (0, 0, -1, -1, 1, 1, -2, -2, 2, 2, -3, -3, 3, 3, 4, 4)
OTHER = (0, 1, 0, 1, 1, 0, 0, 1, 1, 0, 0, 1, 1, 0, 0, 1)


def local(amplitudes, integrals, amp_mask, int_mask):
    z, core, y = (lax.axis_index(name).astype(I32) for name in ("z", "core", "y"))
    near = lax.axis_index("xl") == lax.axis_index("xh")
    up = 1 - 2 * core

    far = (z + up * jnp.asarray(SHIFT, I32)) & 7
    rows = (((far >> 1) - y) & 3) * 4 + (far & 1) * 2 + (core ^ jnp.asarray(OTHER, I32))

    first = pack(amplitudes, amp_mask)
    second = swap(first, "core")
    block = jnp.concatenate([first, second], axis=0)
    held, far_blocks = [block], [swap(block, "xh")]
    for hop in range(1, 5):
        first = lax.ppermute(first, ("z", "core"), RING)
        block = first
        if hop < 4:
            second = lax.ppermute(second, ("z", "core"), RING)
            block = jnp.concatenate([first, second], axis=0)
        held += [block, swap(block, "core")]
        far_blocks.append(swap(block, "xh"))

    def spread(parts):
        return [lax.ppermute(part, "y", [(i, (i + d + 1) % 4) for i in range(4)]) for d, part in enumerate(parts)]

    over = jnp.zeros((META, TILE), I32)
    own_part, *parts, over, kept_ints = chunk_sums(rows, over, integrals, held, int_mask)
    over, *far_blocks[2:] = lax.optimization_barrier((over, *far_blocks[2:]))
    held = far_blocks[:1]
    for block in far_blocks[1:]:
        held += [block, swap(block, "core")]
    sums, coded = zip(add(over, own_part, spread(parts)))
    own_part, *parts, over = chunk_sums(rows, over, kept_ints, held)
    total, sent = add(over, own_part, spread(parts))
    sums, coded = (*sums, total), (*coded, sent)
    near = near.astype(I32).reshape(1)
    sent = choose(near, *coded)
    out, over = last(near, *sums, sent, swap(sent, "xl"))
    return lax.cond(
        jnp.max(over[META - 1]) > 0,
        lambda out: plain(amplitudes, integrals, amp_mask, int_mask),
        lambda out: out,
        out,
    )


def solution(mesh):
    fine = Mesh(mesh.devices.reshape(2, 8, 2, 2, 4), ("xh", "z", "core", "xl", "y"))
    blk, col = ("xh", "z", "core"), ("xl", "y")
    return jax.shard_map(
        local, mesh=fine, in_specs=(P(blk, col),) * 4, out_specs=P(col, blk), check_vma=False
    )
```

```python
import jax
import jax.numpy as jnp
from jax import lax
from jax.experimental import pallas as pl
from jax.experimental.pallas import tpu as pltpu
from jax.sharding import Mesh, PartitionSpec as P

TILE = 128
OWN = 32
TILES = 32
GROUP = 8
WIN = 256
LOW = (0, 80, 240, 320)
ROWS = 576
MSG = ROWS + OWN
RT = 8
META = 16
BIG = 32000.0
F32 = jnp.float32
BF16 = jnp.bfloat16
I16 = jnp.int16
I32 = jnp.int32
VMEM = pl.BlockSpec(memory_space=pltpu.VMEM)
SMEM = pl.BlockSpec(memory_space=pltpu.SMEM)


def swap(x, axis):
    return lax.ppermute(x, axis, [(0, 1), (1, 0)])


def pack_kernel(amps_ref, mask_ref, msg_ref, acc):
    mask = mask_ref[...].astype(F32)
    row = lax.broadcasted_iota(I32, (OWN, OWN), 0)
    col = lax.broadcasted_iota(I32, (OWN, OWN), 1)
    mask16 = mask.astype(BF16)
    in_tile = jnp.dot((col < row).astype(BF16), mask16, preferred_element_type=F32)
    count = jnp.dot(jnp.ones((OWN, OWN), BF16), mask16, preferred_element_type=F32)
    same = row // GROUP == col // GROUP
    before = jnp.dot(count.astype(BF16), ((row < col) & same).astype(BF16), preferred_element_type=F32)
    lane = col // GROUP
    total = [jnp.sum(jnp.where(lane == g, count, 0.0), axis=1, keepdims=True) for g in range(4)]
    start1 = jnp.maximum(total[0], float(LOW[1]))
    end1 = start1 + total[1]
    start3 = ROWS - total[3]
    start2 = jnp.minimum(start3, float(LOW[2] + WIN)) - total[2]
    over = (end1 > LOW[1] + WIN) | (start2 < LOW[2]) | (end1 > start2)
    offset = jnp.where(
        lane == 0,
        0.0,
        jnp.where(lane == 1, start1 - LOW[1], jnp.where(lane == 2, start2 - LOW[2], start3 - LOW[3])),
    )
    place = jnp.where(mask > 0.0, in_tile + before + offset, -1.0)
    over = jnp.broadcast_to(jnp.where(over, 1.0, 0.0), (OWN, TILE - TILES))
    msg_ref[0, ROWS:MSG, :] = jnp.concatenate([place, over], axis=1).astype(BF16)
    acc[...] = jnp.zeros_like(acc)
    spots = lax.broadcasted_iota(I32, (OWN, WIN), 1).astype(F32)
    for g in range(4):
        tiles = range(g * GROUP, (g + 1) * GROUP)
        hot = jnp.concatenate([(place[:, t : t + 1] == spots).astype(BF16) for t in tiles], axis=0)
        val = jnp.concatenate([amps_ref[:, t * TILE : (t + 1) * TILE] for t in tiles], axis=0)
        acc[LOW[g] : LOW[g] + WIN, :] += lax.dot_general(
            hot, val, (((0,), (0,)), ((), ())), preferred_element_type=F32
        )
    msg_ref[0, :ROWS, :] = acc[...].astype(BF16)


def pack(amps, mask):
    return pl.pallas_call(
        pack_kernel,
        out_shape=jax.ShapeDtypeStruct((1, MSG, TILE), BF16),
        scratch_shapes=[pltpu.VMEM((ROWS, TILE), F32)],
        compiler_params=pltpu.CompilerParams(vmem_limit_bytes=8 << 20),
    )(amps, mask)


def code(value):
    most = jnp.max(jnp.abs(value), axis=1, keepdims=True)
    power = jnp.ceil(jnp.log2(jnp.maximum(most, 1e-37)))
    return jnp.round(value * jnp.exp2(-power) * BIG).astype(I32).astype(I16), power


def tile_rows(t):
    return pl.ds(t * TILE, TILE)


def scales(msg_ref):
    powers = msg_ref[RT * TILE :, :].astype(I32).astype(F32)
    return jnp.exp2(jnp.transpose(jnp.concatenate([powers] * (TILE // META), axis=0)))


def decode(msg_ref, scale, t):
    return msg_ref[tile_rows(t), :].astype(I32).astype(F32) * (1.0 / BIG) * scale[:, t : t + 1]


def flags(msg_ref):
    return msg_ref[RT * TILE :, :].astype(I32)


def powers_and_flags(powers, flag):
    row = lax.broadcasted_iota(I32, (META, TILE), 0)
    powers = jnp.transpose(powers)[:META, :].astype(I32)
    return jnp.where(row < RT, powers, flag).astype(I16)


def chunk_kernel(sizes, mask, row_ref, *refs):
    if mask:
        mask_ref, *refs = refs
    before_ref, ints_ref, *refs = refs
    ins, refs = refs[: len(sizes)], refs[len(sizes) :]
    own_ref, a_ref, b_ref, c_ref, over_ref, *refs = refs
    if mask:
        kept_ref, *refs = refs
    got, amps, held, sem = refs

    def load(j):
        return pltpu.make_async_copy(ints_ref.at[pl.ds(j * 2 * TILE, 2 * TILE), :], held.at[j], sem.at[0, j])

    def store(j):
        return pltpu.make_async_copy(held.at[j], kept_ref.at[pl.ds(j * 2 * TILE, 2 * TILE), :], sem.at[1, j])

    for j in range(RT // 2):
        load(j).start()
    i = 0
    for size, ref in zip(sizes, ins, strict=True):
        got[i : i + size] = ref[...]
        i += size
    spots = lax.broadcasted_iota(I32, (OWN, WIN), 1).astype(F32)

    def unpack(i, over):
        place = got[i, ROWS:MSG, :].astype(F32)
        rows = pl.ds(pl.multiple_of(row_ref[i] * OWN, OWN), OWN)
        for g in range(4):
            tiles = range(g * GROUP, (g + 1) * GROUP)
            hot = jnp.concatenate([(place[:, t : t + 1] == spots).astype(BF16) for t in tiles], axis=0)
            value = jnp.dot(hot, got[i, LOW[g] : LOW[g] + WIN, :], preferred_element_type=F32).astype(BF16)
            for n, t in enumerate(tiles):
                amps[rows, t * TILE : (t + 1) * TILE] = value[n * OWN : (n + 1) * OWN, :]
        return jnp.maximum(over, place[:META, TILE - 1 :])

    over = lax.fori_loop(0, i, unpack, jnp.zeros((META, 1), F32), unroll=4)
    over = jnp.maximum(jnp.broadcast_to(over, (META, TILE)).astype(I32), before_ref[...])
    over_ref[...] = over
    lane = lax.broadcasted_iota(I32, (TILE, TILE), 1)

    def multiply(j, powers):
        load(j).wait()
        if mask:
            for n in range(2):
                for t in range(TILES):
                    kept = jnp.where(mask_ref[2 * j + n, t] > 0, 1.0, 0.0).astype(BF16)
                    part = (j, slice(n * TILE, (n + 1) * TILE), slice(t * TILE, (t + 1) * TILE))
                    held[part] = held[part] * kept
            store(j).start()
        value = lax.dot_general(amps[...], held[j], (((1,), (1,)), ((), ())), preferred_element_type=F32)
        for n in range(2):
            t = 2 * j + n
            own_ref[t] = value[:TILE, n * TILE : (n + 1) * TILE]
            new = []
            for d, out in enumerate((a_ref, b_ref, c_ref)):
                coded, power = code(value[(d + 1) * TILE : (d + 2) * TILE, n * TILE : (n + 1) * TILE])
                out[pl.ds(pl.multiple_of(t * TILE, TILE), TILE), :] = coded
                new.append(jnp.where(lane == t, power, powers[d]))
            powers = tuple(new)
        return powers

    powers = lax.fori_loop(0, RT // 2, multiply, (jnp.zeros((TILE, TILE), F32),) * 3)
    for d, out in enumerate((a_ref, b_ref, c_ref)):
        out[RT * TILE :, :] = powers_and_flags(powers[d], over)
    if mask:
        for j in range(RT // 2):
            store(j).wait()


def chunk_sums(rows, before, ints, messages, mask=None):
    sizes = [m.shape[0] for m in messages]
    masks = [] if mask is None else [mask]
    coded = jax.ShapeDtypeStruct((RT * TILE + META, TILE), I16)
    anywhere = pl.BlockSpec(memory_space=pl.ANY)
    return pl.pallas_call(
        lambda *refs: chunk_kernel(sizes, mask is not None, *refs),
        in_specs=[SMEM] * (1 + len(masks)) + [VMEM, anywhere] + [VMEM] * len(sizes),
        out_specs=[VMEM] * 5 + [anywhere] * len(masks),
        out_shape=[
            jax.ShapeDtypeStruct((RT, TILE, TILE), F32),
            coded,
            coded,
            coded,
            jax.ShapeDtypeStruct((META, TILE), I32),
        ]
        + [jax.ShapeDtypeStruct(ints.shape, BF16)] * len(masks),
        scratch_shapes=[
            pltpu.VMEM((sum(sizes), MSG, TILE), BF16),
            pltpu.VMEM((sum(sizes) * OWN, TILES * TILE), BF16),
            pltpu.VMEM((RT // 2, 2 * TILE, TILES * TILE), BF16),
            pltpu.SemaphoreType.DMA((2, RT // 2)),
        ],
        compiler_params=pltpu.CompilerParams(vmem_limit_bytes=44 << 20),
        cost_estimate=pl.CostEstimate(flops=10_000_000_000, bytes_accessed=16 << 20, transcendentals=0),
    )(rows, *masks, before, ints, *messages)


def add_kernel(over_ref, own_ref, a_ref, b_ref, c_ref, sum_ref, out_ref):
    lane = lax.broadcasted_iota(I32, (TILE, TILE), 1)
    parts = (a_ref, b_ref, c_ref)
    scale = [scales(ref) for ref in parts]
    powers = jnp.zeros((TILE, TILE), F32)
    for t in range(RT):
        value = own_ref[t]
        for ref, by in zip(parts, scale, strict=True):
            value = value + decode(ref, by, t)
        sum_ref[t] = value
        out_ref[tile_rows(t), :], power = code(value)
        powers = jnp.where(lane == t, power, powers)
    flag = over_ref[...]
    for ref in parts:
        flag = jnp.maximum(flag, jnp.broadcast_to(flags(ref)[META - 1 :, :], (META, TILE)))
    out_ref[RT * TILE :, :] = powers_and_flags(powers, flag)


def add(over, own, parts):
    return pl.pallas_call(
        add_kernel,
        in_specs=[VMEM] * 5,
        out_specs=[VMEM] * 2,
        out_shape=[
            jax.ShapeDtypeStruct(own.shape, F32),
            jax.ShapeDtypeStruct((RT * TILE + META, TILE), I16),
        ],
        compiler_params=pltpu.CompilerParams(vmem_limit_bytes=8 << 20),
    )(over, own, *parts)


def choose_kernel(near_ref, first_ref, second_ref, out_ref):
    near = near_ref[0] > 0
    both = RT * TILE
    out_ref[:both, :] = jnp.where(near, second_ref[:both, :].astype(I32), first_ref[:both, :].astype(I32)).astype(I16)
    first, second = flags(first_ref), flags(second_ref)
    row = lax.broadcasted_iota(I32, (META, TILE), 0)
    out_ref[both:, :] = jnp.where((row >= RT) | near, second, first).astype(I16)


def choose(near, first, second):
    return pl.pallas_call(
        choose_kernel,
        in_specs=[SMEM] + [VMEM] * 2,
        out_specs=VMEM,
        out_shape=jax.ShapeDtypeStruct(first.shape, I16),
        compiler_params=pltpu.CompilerParams(vmem_limit_bytes=8 << 20),
    )(near, first, second)


def last_kernel(near_ref, first_ref, second_ref, sent_ref, got_ref, out_ref, over_ref):
    near = near_ref[0] > 0
    scale = scales(got_ref)
    for t in range(RT):
        mine = jnp.where(near, first_ref[t], second_ref[t])
        out_ref[:, t * TILE : (t + 1) * TILE] = (mine + decode(got_ref, scale, t)).astype(BF16)
    over_ref[0] = jnp.max(jnp.maximum(flags(sent_ref), flags(got_ref))[RT:, :])


def last(near, first, second, sent, got):
    return pl.pallas_call(
        last_kernel,
        in_specs=[SMEM] + [VMEM] * 4,
        out_specs=[VMEM, SMEM],
        out_shape=[jax.ShapeDtypeStruct((TILE, RT * TILE), BF16), jax.ShapeDtypeStruct((1,), I32)],
        compiler_params=pltpu.CompilerParams(vmem_limit_bytes=8 << 20),
    )(near, first, second, sent, got)


def plain(amplitudes, integrals, amp_mask, int_mask):
    kept = (
        amplitudes.reshape(OWN, TILES, TILE) * amp_mask.astype(BF16)[:, :, None]
    ).reshape(OWN, TILES * TILE)
    copies = jnp.broadcast_to(kept, (32,) + kept.shape)
    every = lax.all_to_all(copies, ("xh", "z", "core"), 0, 0).reshape(32 * OWN, TILES * TILE)
    ints = (
        integrals.reshape(RT, TILE, TILES, TILE) * int_mask.astype(BF16)[:, None, :, None]
    ).reshape(integrals.shape)
    value = lax.dot_general(every, ints, (((1,), (1,)), ((), ())), preferred_element_type=F32)
    parts = lax.all_to_all(value.reshape(8, TILE, RT * TILE), ("xl", "y"), 0, 0)
    return jnp.sum(parts, axis=0).astype(BF16)


RING = [(2 * z, 2 * ((z + 1) % 8)) for z in range(8)] + [(2 * z + 1, 2 * ((z + 7) % 8) + 1) for z in range(8)]

SHIFT = (0, 0, -1, -1, -2, -2, 1, 1, 2, 2, -3, -3, 4, 3, 3, 4)
OTHER = (0, 1, 0, 1, 0, 1, 1, 0, 1, 0, 0, 1, 0, 1, 0, 1)


def local(amplitudes, integrals, amp_mask, int_mask):
    z, core, y = (lax.axis_index(name).astype(I32) for name in ("z", "core", "y"))
    near = lax.axis_index("xl") == lax.axis_index("xh")
    up = 1 - 2 * core

    far = (z + up * jnp.asarray(SHIFT, I32)) & 7
    rows = (((far >> 1) - y) & 3) * 4 + (far & 1) * 2 + (core ^ jnp.asarray(OTHER, I32))

    own = pack(amplitudes, amp_mask)
    across = swap(own, "xh")
    blocks = [[jnp.concatenate([message, swap(message, "core")], axis=0)] for message in (own, across)]
    for hop in range(1, 5):
        for chain in blocks:
            chain.append(lax.ppermute(chain[-1] if hop < 4 else chain[-1][:1], ("z", "core"), RING))
    two = [jnp.concatenate(chain[1:3], axis=0) for chain in blocks]
    rest = jnp.concatenate(blocks[0][3:], axis=0)

    def spread(parts):
        return [lax.ppermute(part, "y", [(i, (i + d + 1) % 4) for i in range(4)]) for d, part in enumerate(parts)]

    over = jnp.zeros((META, TILE), I32)
    held = [blocks[0][0], two[0], swap(two[0], "core"), rest, swap(rest, "core")]
    own_part, *parts, over, kept_ints = chunk_sums(rows, over, integrals, held, int_mask)
    over, late = lax.optimization_barrier((over, blocks[1][4]))
    rest = jnp.concatenate([blocks[1][3], late], axis=0)
    held = [blocks[1][0], two[1], swap(two[1], "core"), rest, swap(rest, "core")]
    sums, coded = zip(add(over, own_part, spread(parts)))
    own_part, *parts, over = chunk_sums(rows, over, kept_ints, held)
    total, sent = add(over, own_part, spread(parts))
    sums, coded = (*sums, total), (*coded, sent)
    near = near.astype(I32).reshape(1)
    sent = choose(near, *coded)
    out, over = last(near, *sums, sent, swap(sent, "xl"))
    return lax.cond(
        over[0] > 0,
        lambda out: plain(amplitudes, integrals, amp_mask, int_mask),
        lambda out: out,
        out,
    )


def solution(mesh):
    fine = Mesh(mesh.devices.reshape(2, 8, 2, 2, 4), ("xh", "z", "core", "xl", "y"))
    blk, col = ("xh", "z", "core"), ("xl", "y")
    return jax.shard_map(
        local, mesh=fine, in_specs=(P(blk, col),) * 4, out_specs=P(col, blk), check_vma=False
    )
```

```python
import jax
import jax.numpy as jnp
from jax import lax
from jax.experimental import pallas as pl
from jax.experimental.pallas import tpu as pltpu
from jax.sharding import Mesh, PartitionSpec as P

TILE = 128
OWN = 32
TILES = 32
GROUP = 8
WIN = 256
LOW = (0, 80, 240, 320)
ROWS = 576
MSG = ROWS + OWN
RT = 8
META = 16
BIG = 32000.0
F32 = jnp.float32
BF16 = jnp.bfloat16
I16 = jnp.int16
I32 = jnp.int32
VMEM = pl.BlockSpec(memory_space=pltpu.VMEM)
SMEM = pl.BlockSpec(memory_space=pltpu.SMEM)


def swap(x, axis):
    return lax.ppermute(x, axis, [(0, 1), (1, 0)])


def pack_kernel(amps_ref, mask_ref, msg_ref, acc):
    mask = mask_ref[...].astype(F32)
    row = lax.broadcasted_iota(I32, (OWN, OWN), 0)
    col = lax.broadcasted_iota(I32, (OWN, OWN), 1)
    mask16 = mask.astype(BF16)
    in_tile = jnp.dot((col < row).astype(BF16), mask16, preferred_element_type=F32)
    count = jnp.dot(jnp.ones((OWN, OWN), BF16), mask16, preferred_element_type=F32)
    same = row // GROUP == col // GROUP
    before = jnp.dot(count.astype(BF16), ((row < col) & same).astype(BF16), preferred_element_type=F32)
    lane = col // GROUP
    total = [jnp.sum(jnp.where(lane == g, count, 0.0), axis=1, keepdims=True) for g in range(4)]
    start1 = jnp.maximum(total[0], float(LOW[1]))
    end1 = start1 + total[1]
    start3 = ROWS - total[3]
    start2 = jnp.minimum(start3, float(LOW[2] + WIN)) - total[2]
    over = (end1 > LOW[1] + WIN) | (start2 < LOW[2]) | (end1 > start2)
    offset = jnp.where(
        lane == 0,
        0.0,
        jnp.where(lane == 1, start1 - LOW[1], jnp.where(lane == 2, start2 - LOW[2], start3 - LOW[3])),
    )
    place = jnp.where(mask > 0.0, in_tile + before + offset, -1.0)
    over = jnp.broadcast_to(jnp.where(over, 1.0, 0.0), (OWN, TILE - TILES))
    msg_ref[0, ROWS:MSG, :] = jnp.concatenate([place, over], axis=1).astype(BF16)
    acc[...] = jnp.zeros_like(acc)
    spots = lax.broadcasted_iota(I32, (OWN, WIN), 1).astype(F32)
    for g in range(4):
        tiles = range(g * GROUP, (g + 1) * GROUP)
        hot = jnp.concatenate([(place[:, t : t + 1] == spots).astype(BF16) for t in tiles], axis=0)
        val = jnp.concatenate([amps_ref[:, t * TILE : (t + 1) * TILE] for t in tiles], axis=0)
        acc[LOW[g] : LOW[g] + WIN, :] += lax.dot_general(
            hot, val, (((0,), (0,)), ((), ())), preferred_element_type=F32
        )
    msg_ref[0, :ROWS, :] = acc[...].astype(BF16)


def pack(amps, mask):
    return pl.pallas_call(
        pack_kernel,
        out_shape=jax.ShapeDtypeStruct((1, MSG, TILE), BF16),
        scratch_shapes=[pltpu.VMEM((ROWS, TILE), F32)],
        compiler_params=pltpu.CompilerParams(vmem_limit_bytes=8 << 20),
    )(amps, mask)


def code(value):
    most = jnp.max(jnp.abs(value), axis=1, keepdims=True)
    power = jnp.ceil(jnp.log2(jnp.maximum(most, 1e-37)))
    return jnp.round(value * jnp.exp2(-power) * BIG).astype(I32).astype(I16), power


def tile_rows(t):
    return pl.ds(t * TILE, TILE)


def scales(msg_ref):
    powers = msg_ref[msg_ref.shape[0] - META :, :].astype(I32).astype(F32)
    return jnp.exp2(jnp.transpose(jnp.concatenate([powers] * (TILE // META), axis=0)))


def decode(msg_ref, scale, t):
    return msg_ref[tile_rows(t), :].astype(I32).astype(F32) * (1.0 / BIG) * scale[:, t : t + 1]


def flags(msg_ref):
    return msg_ref[msg_ref.shape[0] - META :, :].astype(I32)


def powers_and_flags(powers, flag):
    row = lax.broadcasted_iota(I32, (META, TILE), 0)
    powers = jnp.transpose(powers)[:META, :].astype(I32)
    return jnp.where(row < RT, powers, flag).astype(I16)


def unpack_all(sizes, row_ref, ins, got, amps):
    i = 0
    for size, ref in zip(sizes, ins, strict=True):
        got[i : i + size] = ref[...]
        i += size
    spots = lax.broadcasted_iota(I32, (OWN, WIN), 1).astype(F32)

    def unpack(i, over):
        place = got[i, ROWS:MSG, :].astype(F32)
        rows = pl.ds(pl.multiple_of(row_ref[i] * OWN, OWN), OWN)
        for g in range(4):
            tiles = range(g * GROUP, (g + 1) * GROUP)
            hot = jnp.concatenate([(place[:, t : t + 1] == spots).astype(BF16) for t in tiles], axis=0)
            value = jnp.dot(hot, got[i, LOW[g] : LOW[g] + WIN, :], preferred_element_type=F32).astype(BF16)
            for n, t in enumerate(tiles):
                amps[rows, t * TILE : (t + 1) * TILE] = value[n * OWN : (n + 1) * OWN, :]
        return jnp.maximum(over, place[:META, TILE - 1 :])

    over = lax.fori_loop(0, i, unpack, jnp.zeros((META, 1), F32), unroll=4)
    return jnp.broadcast_to(over, (META, TILE)).astype(I32)


def block_copy(ints_ref, held, sem, low):
    return lambda j: pltpu.make_async_copy(
        ints_ref.at[pl.ds((low + j) * 2 * TILE, 2 * TILE), :], held.at[j], sem.at[j]
    )


def multiply_all(amps, held, load, over, own_ref, coded_refs, prepare=None):
    lane = lax.broadcasted_iota(I32, (TILE, TILE), 1)

    def multiply(j, powers):
        load(j).wait()
        if prepare is not None:
            prepare(j)
        value = lax.dot_general(amps[...], held[j], (((1,), (1,)), ((), ())), preferred_element_type=F32)
        for n in range(2):
            t = 2 * j + n
            own_ref[t] = value[:TILE, n * TILE : (n + 1) * TILE]
            new = []
            for d, out in enumerate(coded_refs):
                coded, power = code(value[(d + 1) * TILE : (d + 2) * TILE, n * TILE : (n + 1) * TILE])
                out[pl.ds(pl.multiple_of(t * TILE, TILE), TILE), :] = coded
                new.append(jnp.where(lane == t, power, powers[d]))
            powers = tuple(new)
        return powers

    powers = lax.fori_loop(0, held.shape[0], multiply, (jnp.zeros((TILE, TILE), F32),) * 3)
    for d, out in enumerate(coded_refs):
        out[out.shape[0] - META :, :] = powers_and_flags(powers[d], over)


def first_kernel(sizes, row_ref, mask_ref, ints_ref, *refs):
    ins, refs = refs[: len(sizes)], refs[len(sizes) :]
    own_ref, a_ref, b_ref, c_ref, over_ref, kept_ref, got, amps, held, sem, kept_sem = refs
    load = block_copy(ints_ref, held, sem, 0)
    blocks = held.shape[0]
    for j in range(blocks):
        load(j).start()

    def store(j):
        return pltpu.make_async_copy(held.at[j], kept_ref.at[pl.ds(j * 2 * TILE, 2 * TILE), :], kept_sem.at[j])

    def prepare(j):
        for n in range(2):
            for t in range(TILES):
                kept = jnp.where(mask_ref[2 * j + n, t] > 0, 1.0, 0.0).astype(BF16)
                part = (j, slice(n * TILE, (n + 1) * TILE), slice(t * TILE, (t + 1) * TILE))
                held[part] = held[part] * kept
        store(j).start()

    over = unpack_all(sizes, row_ref, ins, got, amps)
    over_ref[...] = over
    multiply_all(amps, held, load, over, own_ref, (a_ref, b_ref, c_ref), prepare)
    for j in range(blocks):
        store(j).wait()


def second_kernel(sizes, row_ref, before_ref, ints_ref, *refs):
    ins, refs = refs[: len(sizes)], refs[len(sizes) :]
    own_ref, a_ref, b_ref, c_ref, over_ref, amps, got, held, sem = refs
    load = block_copy(ints_ref, held, sem, 0)
    for j in range(held.shape[0]):
        load(j).start()
    over = jnp.maximum(unpack_all(sizes, row_ref, ins, got, amps), before_ref[...])
    over_ref[...] = over
    multiply_all(amps, held, load, over, own_ref, (a_ref, b_ref, c_ref))


def third_kernel(over_ref, ints_ref, amps, own_ref, a_ref, b_ref, c_ref, held, sem):
    load = block_copy(ints_ref, held, sem, held.shape[0])
    for j in range(held.shape[0]):
        load(j).start()
    multiply_all(amps, held, load, over_ref[...], own_ref, (a_ref, b_ref, c_ref))


ANYWHERE = pl.BlockSpec(memory_space=pl.ANY)
FLAGS = jax.ShapeDtypeStruct((META, TILE), I32)
AMPS = (16 * OWN, TILES * TILE)


def sums_of(tiles):
    coded = jax.ShapeDtypeStruct((tiles * TILE + META, TILE), I16)
    return [jax.ShapeDtypeStruct((tiles, TILE, TILE), F32), coded, coded, coded]


def work(tiles):
    return {
        "compiler_params": pltpu.CompilerParams(vmem_limit_bytes=44 << 20),
        "cost_estimate": pl.CostEstimate(
            flops=tiles * 1_250_000_000, bytes_accessed=tiles * (2 << 20), transcendentals=0
        ),
    }


def held_blocks(tiles):
    return pltpu.VMEM((tiles // 2, 2 * TILE, TILES * TILE), BF16)


def first_chunk(rows, mask, ints, messages):
    sizes = [m.shape[0] for m in messages]
    return pl.pallas_call(
        lambda *refs: first_kernel(sizes, *refs),
        in_specs=[SMEM, SMEM, ANYWHERE] + [VMEM] * len(sizes),
        out_specs=[VMEM] * 5 + [ANYWHERE],
        out_shape=[*sums_of(RT), FLAGS, jax.ShapeDtypeStruct(ints.shape, BF16)],
        scratch_shapes=[
            pltpu.VMEM((sum(sizes), MSG, TILE), BF16),
            pltpu.VMEM(AMPS, BF16),
            held_blocks(RT),
            pltpu.SemaphoreType.DMA((RT // 2,)),
            pltpu.SemaphoreType.DMA((RT // 2,)),
        ],
        **work(RT),
    )(rows, mask, ints, *messages)


def second_chunk(rows, before, ints, messages):
    sizes = [m.shape[0] for m in messages]
    return pl.pallas_call(
        lambda *refs: second_kernel(sizes, *refs),
        in_specs=[SMEM, VMEM, ANYWHERE] + [VMEM] * len(sizes),
        out_specs=[VMEM] * 6,
        out_shape=[*sums_of(RT // 2), FLAGS, jax.ShapeDtypeStruct(AMPS, BF16)],
        scratch_shapes=[
            pltpu.VMEM((sum(sizes), MSG, TILE), BF16),
            held_blocks(RT // 2),
            pltpu.SemaphoreType.DMA((RT // 4,)),
        ],
        **work(RT // 2),
    )(rows, before, ints, *messages)


def second_half(over, ints, amps):
    return pl.pallas_call(
        third_kernel,
        in_specs=[VMEM, ANYWHERE, VMEM],
        out_specs=[VMEM] * 4,
        out_shape=sums_of(RT // 2),
        scratch_shapes=[held_blocks(RT // 2), pltpu.SemaphoreType.DMA((RT // 4,))],
        **work(RT // 2),
    )(over, ints, amps)


def add_kernel(over_ref, own_ref, a_ref, b_ref, c_ref, sum_ref, *outs):
    lane = lax.broadcasted_iota(I32, (TILE, TILE), 1)
    parts = (a_ref, b_ref, c_ref)
    scale = [scales(ref) for ref in parts]
    flag = over_ref[...]
    for ref in parts:
        flag = jnp.maximum(flag, jnp.broadcast_to(flags(ref)[META - 1 :, :], (META, TILE)))
    each = own_ref.shape[0] // len(outs)
    for n, out in enumerate(outs):
        powers = jnp.zeros((TILE, TILE), F32)
        for i in range(each):
            t = n * each + i
            value = own_ref[t]
            for ref, by in zip(parts, scale, strict=True):
                value = value + decode(ref, by, t)
            sum_ref[t] = value
            out[tile_rows(i), :], power = code(value)
            powers = jnp.where(lane == i, power, powers)
        out[each * TILE :, :] = powers_and_flags(powers, flag)


def add(over, own, parts, pieces):
    coded = jax.ShapeDtypeStruct((RT // 2 * TILE + META, TILE), I16)
    return pl.pallas_call(
        add_kernel,
        in_specs=[VMEM] * 5,
        out_specs=[VMEM] * (1 + pieces),
        out_shape=[jax.ShapeDtypeStruct(own.shape, F32)] + [coded] * pieces,
        compiler_params=pltpu.CompilerParams(vmem_limit_bytes=8 << 20),
    )(over, own, *parts)


def choose_kernel(near_ref, first_ref, second_ref, out_ref):
    near = near_ref[0] > 0
    both = first_ref.shape[0] - META
    out_ref[:both, :] = jnp.where(near, second_ref[:both, :].astype(I32), first_ref[:both, :].astype(I32)).astype(I16)
    first, second = flags(first_ref), flags(second_ref)
    row = lax.broadcasted_iota(I32, (META, TILE), 0)
    out_ref[both:, :] = jnp.where((row >= RT) | near, second, first).astype(I16)


def choose(near, first, second):
    return pl.pallas_call(
        choose_kernel,
        in_specs=[SMEM] + [VMEM] * 2,
        out_specs=VMEM,
        out_shape=jax.ShapeDtypeStruct(first.shape, I16),
        compiler_params=pltpu.CompilerParams(vmem_limit_bytes=8 << 20),
    )(near, first, second)


def last_kernel(near_ref, first_ref, second_a, second_b, sent_ref, got_a, got_b, out_ref, over_ref):
    near = near_ref[0] > 0
    half = RT // 2
    for n, (second_ref, got_ref) in enumerate(((second_a, got_a), (second_b, got_b))):
        scale = scales(got_ref)
        for i in range(half):
            t = n * half + i
            mine = jnp.where(near, first_ref[t], second_ref[i])
            out_ref[:, t * TILE : (t + 1) * TILE] = (mine + decode(got_ref, scale, i)).astype(BF16)
    over_ref[0] = jnp.max(jnp.maximum(flags(sent_ref), flags(got_b))[RT:, :])


def last(near, first, seconds, sent, got):
    return pl.pallas_call(
        last_kernel,
        in_specs=[SMEM] + [VMEM] * 6,
        out_specs=[VMEM, SMEM],
        out_shape=[jax.ShapeDtypeStruct((TILE, RT * TILE), BF16), jax.ShapeDtypeStruct((1,), I32)],
        compiler_params=pltpu.CompilerParams(vmem_limit_bytes=8 << 20),
    )(near, first, *seconds, sent, *got)


def plain(amplitudes, integrals, amp_mask, int_mask):
    kept = (
        amplitudes.reshape(OWN, TILES, TILE) * amp_mask.astype(BF16)[:, :, None]
    ).reshape(OWN, TILES * TILE)
    copies = jnp.broadcast_to(kept, (32,) + kept.shape)
    every = lax.all_to_all(copies, ("xh", "z", "core"), 0, 0).reshape(32 * OWN, TILES * TILE)
    ints = (
        integrals.reshape(RT, TILE, TILES, TILE) * int_mask.astype(BF16)[:, None, :, None]
    ).reshape(integrals.shape)
    value = lax.dot_general(every, ints, (((1,), (1,)), ((), ())), preferred_element_type=F32)
    parts = lax.all_to_all(value.reshape(8, TILE, RT * TILE), ("xl", "y"), 0, 0)
    return jnp.sum(parts, axis=0).astype(BF16)


RING = [(2 * z, 2 * ((z + 1) % 8)) for z in range(8)] + [(2 * z + 1, 2 * ((z + 7) % 8) + 1) for z in range(8)]

SHIFT = (0, 0, -1, -1, -2, -2, 1, 1, 2, 2, -3, -3, 4, 3, 3, 4)
OTHER = (0, 1, 0, 1, 0, 1, 1, 0, 1, 0, 0, 1, 0, 1, 0, 1)


def local(amplitudes, integrals, amp_mask, int_mask):
    z, core, y = (lax.axis_index(name).astype(I32) for name in ("z", "core", "y"))
    near = lax.axis_index("xl") == lax.axis_index("xh")
    up = 1 - 2 * core

    far = (z + up * jnp.asarray(SHIFT, I32)) & 7
    rows = (((far >> 1) - y) & 3) * 4 + (far & 1) * 2 + (core ^ jnp.asarray(OTHER, I32))

    own = pack(amplitudes, amp_mask)

    def hop(block):
        return lax.ppermute(block, ("z", "core"), RING)

    def with_sibling(message):
        return jnp.concatenate([message, swap(message, "core")], axis=0)

    near_chain = [with_sibling(own)]
    first, far_pair = lax.optimization_barrier((hop(near_chain[0]), with_sibling(swap(own, "xh"))))
    second, far_first = lax.optimization_barrier((hop(first), hop(far_pair)))
    third, far_second = lax.optimization_barrier((hop(second), hop(far_first)))
    near_chain += [first, second, third]
    opposite = hop(third[:1])
    far_chain = [far_pair, far_first, far_second, hop(far_second)]
    blocks = [near_chain, far_chain]
    opposite_across = swap(opposite, "xh")
    two = [jnp.concatenate(chain[1:3], axis=0) for chain in blocks]
    rest = jnp.concatenate([blocks[0][3], opposite], axis=0)

    def spread(parts):
        return [lax.ppermute(part, "y", [(i, (i + d + 1) % 4) for i in range(4)]) for d, part in enumerate(parts)]

    held = [blocks[0][0], two[0], swap(two[0], "core"), rest, swap(rest, "core")]
    own_part, *parts, over, kept_ints = first_chunk(rows, int_mask, integrals, held)
    over, *late = lax.optimization_barrier((over, blocks[1][3], opposite_across))
    rest = jnp.concatenate(late, axis=0)
    held = [blocks[1][0], two[1], swap(two[1], "core"), rest, swap(rest, "core")]
    first_sum, *first_coded = add(over, own_part, spread(parts), 2)

    near = near.astype(I32).reshape(1)
    seconds, got = [], []
    own_part, *parts, over, amps = second_chunk(rows, over, kept_ints, held)
    for half in range(2):
        if half == 1:
            own_part, *parts = second_half(over, kept_ints, amps)
        total, coded = add(over, own_part, spread(parts), 1)
        sent = choose(near, first_coded[half], coded)
        seconds.append(total)
        got.append(swap(sent, "xl"))
    out, over = last(near, first_sum, seconds, sent, got)
    return lax.cond(
        over[0] > 0,
        lambda out: plain(amplitudes, integrals, amp_mask, int_mask),
        lambda out: out,
        out,
    )


def solution(mesh):
    fine = Mesh(mesh.devices.reshape(2, 8, 2, 2, 4), ("xh", "z", "core", "xl", "y"))
    blk, col = ("xh", "z", "core"), ("xl", "y")
    return jax.shard_map(
        local, mesh=fine, in_specs=(P(blk, col),) * 4, out_specs=P(col, blk), check_vma=False
    )
```

```python
import jax
import jax.numpy as jnp
from jax import lax
from jax.experimental import pallas as pl
from jax.experimental.pallas import tpu as pltpu
from jax.sharding import Mesh, PartitionSpec as P

TILE = 128
OWN = 32
TILES = 32
GROUP = 8
WIN = 256
LOW = (0, 80, 240, 320)
ROWS = 576
MSG = ROWS + OWN
RT = 8
META = 16
BIG = 32000.0
F32 = jnp.float32
BF16 = jnp.bfloat16
I16 = jnp.int16
I32 = jnp.int32
VMEM = pl.BlockSpec(memory_space=pltpu.VMEM)
SMEM = pl.BlockSpec(memory_space=pltpu.SMEM)


def swap(x, axis):
    return lax.ppermute(x, axis, [(0, 1), (1, 0)])


def pack_kernel(amps_ref, mask_ref, msg_ref, acc):
    mask = mask_ref[...].astype(F32)
    row = lax.broadcasted_iota(I32, (OWN, OWN), 0)
    col = lax.broadcasted_iota(I32, (OWN, OWN), 1)
    mask16 = mask.astype(BF16)
    in_tile = jnp.dot((col < row).astype(BF16), mask16, preferred_element_type=F32)
    count = jnp.dot(jnp.ones((OWN, OWN), BF16), mask16, preferred_element_type=F32)
    same = row // GROUP == col // GROUP
    before = jnp.dot(count.astype(BF16), ((row < col) & same).astype(BF16), preferred_element_type=F32)
    lane = col // GROUP
    total = [jnp.sum(jnp.where(lane == g, count, 0.0), axis=1, keepdims=True) for g in range(4)]
    start1 = jnp.maximum(total[0], float(LOW[1]))
    end1 = start1 + total[1]
    start3 = ROWS - total[3]
    start2 = jnp.minimum(start3, float(LOW[2] + WIN)) - total[2]
    over = (end1 > LOW[1] + WIN) | (start2 < LOW[2]) | (end1 > start2)
    offset = jnp.where(
        lane == 0,
        0.0,
        jnp.where(lane == 1, start1 - LOW[1], jnp.where(lane == 2, start2 - LOW[2], start3 - LOW[3])),
    )
    place = jnp.where(mask > 0.0, in_tile + before + offset, -1.0)
    over = jnp.broadcast_to(jnp.where(over, 1.0, 0.0), (OWN, TILE - TILES))
    msg_ref[0, ROWS:MSG, :] = jnp.concatenate([place, over], axis=1).astype(BF16)
    acc[...] = jnp.zeros_like(acc)
    spots = lax.broadcasted_iota(I32, (OWN, WIN), 1).astype(F32)
    for g in range(4):
        tiles = range(g * GROUP, (g + 1) * GROUP)
        hot = jnp.concatenate([(place[:, t : t + 1] == spots).astype(BF16) for t in tiles], axis=0)
        val = jnp.concatenate([amps_ref[:, t * TILE : (t + 1) * TILE] for t in tiles], axis=0)
        acc[LOW[g] : LOW[g] + WIN, :] += lax.dot_general(
            hot, val, (((0,), (0,)), ((), ())), preferred_element_type=F32
        )
    msg_ref[0, :ROWS, :] = acc[...].astype(BF16)


def pack(amps, mask):
    return pl.pallas_call(
        pack_kernel,
        out_shape=jax.ShapeDtypeStruct((1, MSG, TILE), BF16),
        scratch_shapes=[pltpu.VMEM((ROWS, TILE), F32)],
        compiler_params=pltpu.CompilerParams(vmem_limit_bytes=8 << 20),
    )(amps, mask)


def code(value):
    most = jnp.max(jnp.abs(value), axis=1, keepdims=True)
    power = jnp.ceil(jnp.log2(jnp.maximum(most, 1e-37)))
    return jnp.round(value * jnp.exp2(-power) * BIG).astype(I32).astype(I16), power


def tile_rows(t):
    return pl.ds(t * TILE, TILE)


def scales(msg_ref):
    powers = msg_ref[msg_ref.shape[0] - META :, :].astype(I32).astype(F32)
    return jnp.exp2(jnp.transpose(jnp.concatenate([powers] * (TILE // META), axis=0)))


def decode(msg_ref, scale, t):
    return msg_ref[tile_rows(t), :].astype(I32).astype(F32) * (1.0 / BIG) * scale[:, t : t + 1]


def flags(msg_ref):
    return msg_ref[msg_ref.shape[0] - META :, :].astype(I32)


def powers_and_flags(powers, flag):
    row = lax.broadcasted_iota(I32, (META, TILE), 0)
    powers = jnp.transpose(powers)[:META, :].astype(I32)
    return jnp.where(row < RT, powers, flag).astype(I16)


def unpack_all(sizes, row_ref, ins, got, amps):
    i = 0
    for size, ref in zip(sizes, ins, strict=True):
        got[i : i + size] = ref[...]
        i += size
    spots = lax.broadcasted_iota(I32, (OWN, WIN), 1).astype(F32)

    def unpack(i, over):
        place = got[i, ROWS:MSG, :].astype(F32)
        rows = pl.ds(pl.multiple_of(row_ref[i] * OWN, OWN), OWN)
        for g in range(4):
            tiles = range(g * GROUP, (g + 1) * GROUP)
            hot = jnp.concatenate([(place[:, t : t + 1] == spots).astype(BF16) for t in tiles], axis=0)
            value = jnp.dot(hot, got[i, LOW[g] : LOW[g] + WIN, :], preferred_element_type=F32).astype(BF16)
            for n, t in enumerate(tiles):
                amps[rows, t * TILE : (t + 1) * TILE] = value[n * OWN : (n + 1) * OWN, :]
        return jnp.maximum(over, place[:META, TILE - 1 :])

    over = lax.fori_loop(0, i, unpack, jnp.zeros((META, 1), F32), unroll=4)
    return jnp.broadcast_to(over, (META, TILE)).astype(I32)


def block_copy(ints_ref, held, sem, low):
    return lambda j: pltpu.make_async_copy(
        ints_ref.at[pl.ds((low + j) * 2 * TILE, 2 * TILE), :], held.at[j], sem.at[j]
    )


def multiply_all(amps, held, load, over, own_ref, coded_refs, prepare=None):
    lane = lax.broadcasted_iota(I32, (TILE, TILE), 1)

    def multiply(j, powers):
        load(j).wait()
        if prepare is not None:
            prepare(j)
        value = lax.dot_general(amps[...], held[j], (((1,), (1,)), ((), ())), preferred_element_type=F32)
        for n in range(2):
            t = 2 * j + n
            own_ref[t] = value[:TILE, n * TILE : (n + 1) * TILE]
            new = []
            for d, out in enumerate(coded_refs):
                coded, power = code(value[(d + 1) * TILE : (d + 2) * TILE, n * TILE : (n + 1) * TILE])
                out[pl.ds(pl.multiple_of(t * TILE, TILE), TILE), :] = coded
                new.append(jnp.where(lane == t, power, powers[d]))
            powers = tuple(new)
        return powers

    powers = lax.fori_loop(0, held.shape[0], multiply, (jnp.zeros((TILE, TILE), F32),) * 3)
    for d, out in enumerate(coded_refs):
        out[out.shape[0] - META :, :] = powers_and_flags(powers[d], over)


def first_kernel(sizes, row_ref, mask_ref, ints_ref, *refs):
    ins, refs = refs[: len(sizes)], refs[len(sizes) :]
    own_ref, a_ref, b_ref, c_ref, over_ref, kept_ref, got, amps, held, sem, kept_sem = refs
    load = block_copy(ints_ref, held, sem, 0)
    blocks = held.shape[0]
    for j in range(blocks):
        load(j).start()

    def store(j):
        return pltpu.make_async_copy(held.at[j], kept_ref.at[pl.ds(j * 2 * TILE, 2 * TILE), :], kept_sem.at[j])

    def prepare(j):
        for n in range(2):
            for t in range(TILES):
                kept = jnp.where(mask_ref[2 * j + n, t] > 0, 1.0, 0.0).astype(BF16)
                part = (j, slice(n * TILE, (n + 1) * TILE), slice(t * TILE, (t + 1) * TILE))
                held[part] = held[part] * kept
        store(j).start()

    over = unpack_all(sizes, row_ref, ins, got, amps)
    over_ref[...] = over
    multiply_all(amps, held, load, over, own_ref, (a_ref, b_ref, c_ref), prepare)
    for j in range(blocks):
        store(j).wait()


def second_kernel(sizes, row_ref, before_ref, ints_ref, *refs):
    ins, refs = refs[: len(sizes)], refs[len(sizes) :]
    own_ref, a_ref, b_ref, c_ref, over_ref, amps, got, held, sem = refs
    load = block_copy(ints_ref, held, sem, 0)
    for j in range(held.shape[0]):
        load(j).start()
    over = jnp.maximum(unpack_all(sizes, row_ref, ins, got, amps), before_ref[...])
    over_ref[...] = over
    multiply_all(amps, held, load, over, own_ref, (a_ref, b_ref, c_ref))


def third_kernel(over_ref, ints_ref, amps, own_ref, a_ref, b_ref, c_ref, held, sem):
    load = block_copy(ints_ref, held, sem, held.shape[0])
    for j in range(held.shape[0]):
        load(j).start()
    multiply_all(amps, held, load, over_ref[...], own_ref, (a_ref, b_ref, c_ref))


ANYWHERE = pl.BlockSpec(memory_space=pl.ANY)
FLAGS = jax.ShapeDtypeStruct((META, TILE), I32)
AMPS = (16 * OWN, TILES * TILE)


def sums_of(tiles):
    coded = jax.ShapeDtypeStruct((tiles * TILE + META, TILE), I16)
    return [jax.ShapeDtypeStruct((tiles, TILE, TILE), F32), coded, coded, coded]


def work(tiles):
    return {
        "compiler_params": pltpu.CompilerParams(vmem_limit_bytes=44 << 20),
        "cost_estimate": pl.CostEstimate(
            flops=tiles * 1_250_000_000, bytes_accessed=tiles * (2 << 20), transcendentals=0
        ),
    }


def held_blocks(tiles):
    return pltpu.VMEM((tiles // 2, 2 * TILE, TILES * TILE), BF16)


def first_chunk(rows, mask, ints, messages):
    sizes = [m.shape[0] for m in messages]
    return pl.pallas_call(
        lambda *refs: first_kernel(sizes, *refs),
        in_specs=[SMEM, SMEM, ANYWHERE] + [VMEM] * len(sizes),
        out_specs=[VMEM] * 5 + [ANYWHERE],
        out_shape=[*sums_of(RT), FLAGS, jax.ShapeDtypeStruct(ints.shape, BF16)],
        scratch_shapes=[
            pltpu.VMEM((sum(sizes), MSG, TILE), BF16),
            pltpu.VMEM(AMPS, BF16),
            held_blocks(RT),
            pltpu.SemaphoreType.DMA((RT // 2,)),
            pltpu.SemaphoreType.DMA((RT // 2,)),
        ],
        **work(RT),
    )(rows, mask, ints, *messages)


def second_chunk(rows, before, ints, messages):
    sizes = [m.shape[0] for m in messages]
    return pl.pallas_call(
        lambda *refs: second_kernel(sizes, *refs),
        in_specs=[SMEM, VMEM, ANYWHERE] + [VMEM] * len(sizes),
        out_specs=[VMEM] * 6,
        out_shape=[*sums_of(RT // 2), FLAGS, jax.ShapeDtypeStruct(AMPS, BF16)],
        scratch_shapes=[
            pltpu.VMEM((sum(sizes), MSG, TILE), BF16),
            held_blocks(RT // 2),
            pltpu.SemaphoreType.DMA((RT // 4,)),
        ],
        **work(RT // 2),
    )(rows, before, ints, *messages)


def second_half(over, ints, amps):
    return pl.pallas_call(
        third_kernel,
        in_specs=[VMEM, ANYWHERE, VMEM],
        out_specs=[VMEM] * 4,
        out_shape=sums_of(RT // 2),
        scratch_shapes=[held_blocks(RT // 2), pltpu.SemaphoreType.DMA((RT // 4,))],
        **work(RT // 2),
    )(over, ints, amps)


def add_kernel(over_ref, own_ref, a_ref, b_ref, c_ref, sum_ref, *outs):
    lane = lax.broadcasted_iota(I32, (TILE, TILE), 1)
    parts = (a_ref, b_ref, c_ref)
    scale = [scales(ref) for ref in parts]
    flag = over_ref[...]
    for ref in parts:
        flag = jnp.maximum(flag, jnp.broadcast_to(flags(ref)[META - 1 :, :], (META, TILE)))
    each = own_ref.shape[0] // len(outs)
    for n, out in enumerate(outs):
        powers = jnp.zeros((TILE, TILE), F32)
        for i in range(each):
            t = n * each + i
            value = own_ref[t]
            for ref, by in zip(parts, scale, strict=True):
                value = value + decode(ref, by, t)
            sum_ref[t] = value
            out[tile_rows(i), :], power = code(value)
            powers = jnp.where(lane == i, power, powers)
        out[each * TILE :, :] = powers_and_flags(powers, flag)


def add(over, own, parts, pieces):
    coded = jax.ShapeDtypeStruct((RT // 2 * TILE + META, TILE), I16)
    return pl.pallas_call(
        add_kernel,
        in_specs=[VMEM] * 5,
        out_specs=[VMEM] * (1 + pieces),
        out_shape=[jax.ShapeDtypeStruct(own.shape, F32)] + [coded] * pieces,
        compiler_params=pltpu.CompilerParams(vmem_limit_bytes=8 << 20),
    )(over, own, *parts)


def choose_kernel(near_ref, first_ref, second_ref, out_ref):
    near = near_ref[0] > 0
    both = first_ref.shape[0] - META
    out_ref[:both, :] = jnp.where(near, second_ref[:both, :].astype(I32), first_ref[:both, :].astype(I32)).astype(I16)
    first, second = flags(first_ref), flags(second_ref)
    row = lax.broadcasted_iota(I32, (META, TILE), 0)
    out_ref[both:, :] = jnp.where((row >= RT) | near, second, first).astype(I16)


def choose(near, first, second):
    return pl.pallas_call(
        choose_kernel,
        in_specs=[SMEM] + [VMEM] * 2,
        out_specs=VMEM,
        out_shape=jax.ShapeDtypeStruct(first.shape, I16),
        compiler_params=pltpu.CompilerParams(vmem_limit_bytes=8 << 20),
    )(near, first, second)


def last_kernel(near_ref, first_ref, second_a, second_b, sent_ref, got_a, got_b, out_ref, over_ref):
    near = near_ref[0] > 0
    half = RT // 2
    for n, (second_ref, got_ref) in enumerate(((second_a, got_a), (second_b, got_b))):
        scale = scales(got_ref)
        for i in range(half):
            t = n * half + i
            mine = jnp.where(near, first_ref[t], second_ref[i])
            out_ref[:, t * TILE : (t + 1) * TILE] = (mine + decode(got_ref, scale, i)).astype(BF16)
    over_ref[0] = jnp.max(jnp.maximum(flags(sent_ref), flags(got_b))[RT:, :])


def last(near, first, seconds, sent, got):
    return pl.pallas_call(
        last_kernel,
        in_specs=[SMEM] + [VMEM] * 6,
        out_specs=[VMEM, SMEM],
        out_shape=[jax.ShapeDtypeStruct((TILE, RT * TILE), BF16), jax.ShapeDtypeStruct((1,), I32)],
        compiler_params=pltpu.CompilerParams(vmem_limit_bytes=8 << 20),
    )(near, first, *seconds, sent, *got)


def plain(amplitudes, integrals, amp_mask, int_mask):
    kept = (
        amplitudes.reshape(OWN, TILES, TILE) * amp_mask.astype(BF16)[:, :, None]
    ).reshape(OWN, TILES * TILE)
    copies = jnp.broadcast_to(kept, (32,) + kept.shape)
    every = lax.all_to_all(copies, ("xh", "z", "core"), 0, 0).reshape(32 * OWN, TILES * TILE)
    ints = (
        integrals.reshape(RT, TILE, TILES, TILE) * int_mask.astype(BF16)[:, None, :, None]
    ).reshape(integrals.shape)
    value = lax.dot_general(every, ints, (((1,), (1,)), ((), ())), preferred_element_type=F32)
    parts = lax.all_to_all(value.reshape(8, TILE, RT * TILE), ("xl", "y"), 0, 0)
    return jnp.sum(parts, axis=0).astype(BF16)


RING = [(2 * z, 2 * ((z + 1) % 8)) for z in range(8)] + [(2 * z + 1, 2 * ((z + 7) % 8) + 1) for z in range(8)]

SHIFT = (0, 0, -1, -1, -2, -2, 1, 1, 2, 2, -3, -3, 4, 3, 3, 4)
OTHER = (0, 1, 0, 1, 0, 1, 1, 0, 1, 0, 0, 1, 0, 1, 0, 1)


def local(amplitudes, integrals, amp_mask, int_mask):
    z, core, y = (lax.axis_index(name).astype(I32) for name in ("z", "core", "y"))
    near = lax.axis_index("xl") == lax.axis_index("xh")
    up = 1 - 2 * core

    far = (z + up * jnp.asarray(SHIFT, I32)) & 7
    rows = (((far >> 1) - y) & 3) * 4 + (far & 1) * 2 + (core ^ jnp.asarray(OTHER, I32))

    own = pack(amplitudes, amp_mask)
    across = swap(own, "xh")
    blocks = [[jnp.concatenate([message, swap(message, "core")], axis=0)] for message in (own, across)]
    for hop in range(1, 5):
        for chain in blocks:
            chain.append(lax.ppermute(chain[-1] if hop < 4 else chain[-1][:1], ("z", "core"), RING))
    two = [jnp.concatenate(chain[1:3], axis=0) for chain in blocks]
    rest = jnp.concatenate(blocks[0][3:], axis=0)

    def spread(parts):
        return [lax.ppermute(part, "y", [(i, (i + d + 1) % 4) for i in range(4)]) for d, part in enumerate(parts)]

    held = [blocks[0][0], two[0], swap(two[0], "core"), rest, swap(rest, "core")]
    own_part, *parts, over, kept_ints = first_chunk(rows, int_mask, integrals, held)
    over, late = lax.optimization_barrier((over, blocks[1][4]))
    rest = jnp.concatenate([blocks[1][3], late], axis=0)
    held = [blocks[1][0], two[1], swap(two[1], "core"), rest, swap(rest, "core")]
    first_sum, *first_coded = add(over, own_part, spread(parts), 2)

    near = near.astype(I32).reshape(1)
    seconds, got = [], []
    own_part, *parts, over, amps = second_chunk(rows, over, kept_ints, held)
    for half in range(2):
        if half == 1:
            own_part, *parts = second_half(over, kept_ints, amps)
        total, coded = add(over, own_part, spread(parts), 1)
        sent = choose(near, first_coded[half], coded)
        seconds.append(total)
        got.append(swap(sent, "xl"))
    out, over = last(near, first_sum, seconds, sent, got)
    return lax.cond(
        over[0] > 0,
        lambda out: plain(amplitudes, integrals, amp_mask, int_mask),
        lambda out: out,
        out,
    )


def solution(mesh):
    fine = Mesh(mesh.devices.reshape(2, 8, 2, 2, 4), ("xh", "z", "core", "xl", "y"))
    blk, col = ("xh", "z", "core"), ("xl", "y")
    return jax.shard_map(
        local, mesh=fine, in_specs=(P(blk, col),) * 4, out_specs=P(col, blk), check_vma=False
    )
```

```python
import jax
import jax.numpy as jnp
from jax import lax
from jax.experimental import pallas as pl
from jax.experimental.pallas import tpu as pltpu
from jax.sharding import Mesh, PartitionSpec as P

TILE = 128
OWN = 32
TILES = 32
GROUP = 8
WIN = 256
LOW = (0, 80, 240, 320)
ROWS = 576
MSG = ROWS + OWN
RT = 8
META = 16
BIG = 32000.0
F32 = jnp.float32
BF16 = jnp.bfloat16
I16 = jnp.int16
I32 = jnp.int32
VMEM = pl.BlockSpec(memory_space=pltpu.VMEM)
SMEM = pl.BlockSpec(memory_space=pltpu.SMEM)


def swap(x, axis):
    return lax.ppermute(x, axis, [(0, 1), (1, 0)])


def pack_kernel(amps_ref, mask_ref, msg_ref, acc):
    mask = mask_ref[...].astype(F32)
    row = lax.broadcasted_iota(I32, (OWN, OWN), 0)
    col = lax.broadcasted_iota(I32, (OWN, OWN), 1)
    mask16 = mask.astype(BF16)
    in_tile = jnp.dot((col < row).astype(BF16), mask16, preferred_element_type=F32)
    count = jnp.dot(jnp.ones((OWN, OWN), BF16), mask16, preferred_element_type=F32)
    same = row // GROUP == col // GROUP
    before = jnp.dot(count.astype(BF16), ((row < col) & same).astype(BF16), preferred_element_type=F32)
    lane = col // GROUP
    total = [jnp.sum(jnp.where(lane == g, count, 0.0), axis=1, keepdims=True) for g in range(4)]
    start1 = jnp.maximum(total[0], float(LOW[1]))
    end1 = start1 + total[1]
    start3 = ROWS - total[3]
    start2 = jnp.minimum(start3, float(LOW[2] + WIN)) - total[2]
    over = (end1 > LOW[1] + WIN) | (start2 < LOW[2]) | (end1 > start2)
    offset = jnp.where(
        lane == 0,
        0.0,
        jnp.where(lane == 1, start1 - LOW[1], jnp.where(lane == 2, start2 - LOW[2], start3 - LOW[3])),
    )
    place = jnp.where(mask > 0.0, in_tile + before + offset, -1.0)
    over = jnp.broadcast_to(jnp.where(over, 1.0, 0.0), (OWN, TILE - TILES))
    msg_ref[0, ROWS:MSG, :] = jnp.concatenate([place, over], axis=1).astype(BF16)
    acc[...] = jnp.zeros_like(acc)
    spots = lax.broadcasted_iota(I32, (OWN, WIN), 1).astype(F32)
    for g in range(4):
        tiles = range(g * GROUP, (g + 1) * GROUP)
        hot = jnp.concatenate([(place[:, t : t + 1] == spots).astype(BF16) for t in tiles], axis=0)
        val = jnp.concatenate([amps_ref[:, t * TILE : (t + 1) * TILE] for t in tiles], axis=0)
        acc[LOW[g] : LOW[g] + WIN, :] += lax.dot_general(
            hot, val, (((0,), (0,)), ((), ())), preferred_element_type=F32
        )
    msg_ref[0, :ROWS, :] = acc[...].astype(BF16)


def pack(amps, mask):
    return pl.pallas_call(
        pack_kernel,
        out_shape=jax.ShapeDtypeStruct((1, MSG, TILE), BF16),
        scratch_shapes=[pltpu.VMEM((ROWS, TILE), F32)],
        compiler_params=pltpu.CompilerParams(vmem_limit_bytes=8 << 20),
    )(amps, mask)


def code(value):
    most = jnp.max(jnp.abs(value), axis=1, keepdims=True)
    power = jnp.ceil(jnp.log2(jnp.maximum(most, 1e-37)))
    return jnp.round(value * jnp.exp2(-power) * BIG).astype(I32).astype(I16), power


def tile_rows(t):
    return pl.ds(t * TILE, TILE)


def scales(msg_ref):
    powers = msg_ref[msg_ref.shape[0] - META :, :].astype(I32).astype(F32)
    return jnp.exp2(jnp.transpose(jnp.concatenate([powers] * (TILE // META), axis=0)))


def decode(msg_ref, scale, t):
    return msg_ref[tile_rows(t), :].astype(I32).astype(F32) * (1.0 / BIG) * scale[:, t : t + 1]


def flags(msg_ref):
    return msg_ref[msg_ref.shape[0] - META :, :].astype(I32)


def powers_and_flags(powers, flag):
    row = lax.broadcasted_iota(I32, (META, TILE), 0)
    powers = jnp.transpose(powers)[:META, :].astype(I32)
    return jnp.where(row < RT, powers, flag).astype(I16)


def unpack_all(sizes, row_ref, ins, got, amps):
    i = 0
    for size, ref in zip(sizes, ins, strict=True):
        got[i : i + size] = ref[...]
        i += size
    spots = lax.broadcasted_iota(I32, (OWN, WIN), 1).astype(F32)

    def unpack(i, over):
        place = got[i, ROWS:MSG, :].astype(F32)
        rows = pl.ds(pl.multiple_of(row_ref[i] * OWN, OWN), OWN)
        for g in range(4):
            tiles = range(g * GROUP, (g + 1) * GROUP)
            hot = jnp.concatenate([(place[:, t : t + 1] == spots).astype(BF16) for t in tiles], axis=0)
            value = jnp.dot(hot, got[i, LOW[g] : LOW[g] + WIN, :], preferred_element_type=F32).astype(BF16)
            for n, t in enumerate(tiles):
                amps[rows, t * TILE : (t + 1) * TILE] = value[n * OWN : (n + 1) * OWN, :]
        return jnp.maximum(over, place[:META, TILE - 1 :])

    over = lax.fori_loop(0, i, unpack, jnp.zeros((META, 1), F32), unroll=4)
    return jnp.broadcast_to(over, (META, TILE)).astype(I32)


def block_copy(ints_ref, held, sem, low):
    return lambda j: pltpu.make_async_copy(
        ints_ref.at[pl.ds((low + j) * 2 * TILE, 2 * TILE), :], held.at[j], sem.at[j]
    )


def multiply_all(amps, held, load, over, own_ref, coded_refs, prepare=None):
    lane = lax.broadcasted_iota(I32, (TILE, TILE), 1)

    def multiply(j, powers):
        load(j).wait()
        if prepare is not None:
            prepare(j)
        value = lax.dot_general(amps[...], held[j], (((1,), (1,)), ((), ())), preferred_element_type=F32)
        for n in range(2):
            t = 2 * j + n
            own_ref[t] = value[:TILE, n * TILE : (n + 1) * TILE]
            new = []
            for d, out in enumerate(coded_refs):
                coded, power = code(value[(d + 1) * TILE : (d + 2) * TILE, n * TILE : (n + 1) * TILE])
                out[pl.ds(pl.multiple_of(t * TILE, TILE), TILE), :] = coded
                new.append(jnp.where(lane == t, power, powers[d]))
            powers = tuple(new)
        return powers

    powers = lax.fori_loop(0, held.shape[0], multiply, (jnp.zeros((TILE, TILE), F32),) * 3)
    for d, out in enumerate(coded_refs):
        out[out.shape[0] - META :, :] = powers_and_flags(powers[d], over)


def first_kernel(sizes, row_ref, mask_ref, ints_ref, *refs):
    ins, refs = refs[: len(sizes)], refs[len(sizes) :]
    own_ref, a_ref, b_ref, c_ref, over_ref, kept_ref, got, amps, held, sem, kept_sem = refs
    load = block_copy(ints_ref, held, sem, 0)
    blocks = held.shape[0]
    for j in range(blocks):
        load(j).start()

    def store(j):
        return pltpu.make_async_copy(held.at[j], kept_ref.at[pl.ds(j * 2 * TILE, 2 * TILE), :], kept_sem.at[j])

    def prepare(j):
        for n in range(2):
            for t in range(TILES):
                kept = jnp.where(mask_ref[2 * j + n, t] > 0, 1.0, 0.0).astype(BF16)
                part = (j, slice(n * TILE, (n + 1) * TILE), slice(t * TILE, (t + 1) * TILE))
                held[part] = held[part] * kept
        store(j).start()

    over = unpack_all(sizes, row_ref, ins, got, amps)
    over_ref[...] = over
    multiply_all(amps, held, load, over, own_ref, (a_ref, b_ref, c_ref), prepare)
    for j in range(blocks):
        store(j).wait()


def second_kernel(sizes, row_ref, before_ref, ints_ref, *refs):
    ins, refs = refs[: len(sizes)], refs[len(sizes) :]
    own_ref, a_ref, b_ref, c_ref, over_ref, amps, got, held, sem = refs
    load = block_copy(ints_ref, held, sem, 0)
    for j in range(held.shape[0]):
        load(j).start()
    over = jnp.maximum(unpack_all(sizes, row_ref, ins, got, amps), before_ref[...])
    over_ref[...] = over
    multiply_all(amps, held, load, over, own_ref, (a_ref, b_ref, c_ref))


def third_kernel(over_ref, ints_ref, amps, own_ref, a_ref, b_ref, c_ref, held, sem):
    load = block_copy(ints_ref, held, sem, held.shape[0])
    for j in range(held.shape[0]):
        load(j).start()
    multiply_all(amps, held, load, over_ref[...], own_ref, (a_ref, b_ref, c_ref))


ANYWHERE = pl.BlockSpec(memory_space=pl.ANY)
FLAGS = jax.ShapeDtypeStruct((META, TILE), I32)
AMPS = (16 * OWN, TILES * TILE)


def sums_of(tiles):
    coded = jax.ShapeDtypeStruct((tiles * TILE + META, TILE), I16)
    return [jax.ShapeDtypeStruct((tiles, TILE, TILE), F32), coded, coded, coded]


def work(tiles):
    return {
        "compiler_params": pltpu.CompilerParams(vmem_limit_bytes=44 << 20),
        "cost_estimate": pl.CostEstimate(
            flops=tiles * 1_250_000_000, bytes_accessed=tiles * (2 << 20), transcendentals=0
        ),
    }


def held_blocks(tiles):
    return pltpu.VMEM((tiles // 2, 2 * TILE, TILES * TILE), BF16)


def first_chunk(rows, mask, ints, messages):
    sizes = [m.shape[0] for m in messages]
    return pl.pallas_call(
        lambda *refs: first_kernel(sizes, *refs),
        in_specs=[SMEM, SMEM, ANYWHERE] + [VMEM] * len(sizes),
        out_specs=[VMEM] * 5 + [ANYWHERE],
        out_shape=[*sums_of(RT), FLAGS, jax.ShapeDtypeStruct(ints.shape, BF16)],
        scratch_shapes=[
            pltpu.VMEM((sum(sizes), MSG, TILE), BF16),
            pltpu.VMEM(AMPS, BF16),
            held_blocks(RT),
            pltpu.SemaphoreType.DMA((RT // 2,)),
            pltpu.SemaphoreType.DMA((RT // 2,)),
        ],
        **work(RT),
    )(rows, mask, ints, *messages)


def second_chunk(rows, before, ints, messages):
    sizes = [m.shape[0] for m in messages]
    return pl.pallas_call(
        lambda *refs: second_kernel(sizes, *refs),
        in_specs=[SMEM, VMEM, ANYWHERE] + [VMEM] * len(sizes),
        out_specs=[VMEM] * 6,
        out_shape=[*sums_of(RT // 2), FLAGS, jax.ShapeDtypeStruct(AMPS, BF16)],
        scratch_shapes=[
            pltpu.VMEM((sum(sizes), MSG, TILE), BF16),
            held_blocks(RT // 2),
            pltpu.SemaphoreType.DMA((RT // 4,)),
        ],
        **work(RT // 2),
    )(rows, before, ints, *messages)


def second_half(over, ints, amps):
    return pl.pallas_call(
        third_kernel,
        in_specs=[VMEM, ANYWHERE, VMEM],
        out_specs=[VMEM] * 4,
        out_shape=sums_of(RT // 2),
        scratch_shapes=[held_blocks(RT // 2), pltpu.SemaphoreType.DMA((RT // 4,))],
        **work(RT // 2),
    )(over, ints, amps)


def add_kernel(over_ref, own_ref, a_ref, b_ref, c_ref, sum_ref, *outs):
    lane = lax.broadcasted_iota(I32, (TILE, TILE), 1)
    parts = (a_ref, b_ref, c_ref)
    scale = [scales(ref) for ref in parts]
    flag = over_ref[...]
    for ref in parts:
        flag = jnp.maximum(flag, jnp.broadcast_to(flags(ref)[META - 1 :, :], (META, TILE)))
    each = own_ref.shape[0] // len(outs)
    for n, out in enumerate(outs):
        powers = jnp.zeros((TILE, TILE), F32)
        for i in range(each):
            t = n * each + i
            value = own_ref[t]
            for ref, by in zip(parts, scale, strict=True):
                value = value + decode(ref, by, t)
            sum_ref[t] = value
            out[tile_rows(i), :], power = code(value)
            powers = jnp.where(lane == i, power, powers)
        out[each * TILE :, :] = powers_and_flags(powers, flag)


def add(over, own, parts, pieces):
    coded = jax.ShapeDtypeStruct((RT // 2 * TILE + META, TILE), I16)
    return pl.pallas_call(
        add_kernel,
        in_specs=[VMEM] * 5,
        out_specs=[VMEM] * (1 + pieces),
        out_shape=[jax.ShapeDtypeStruct(own.shape, F32)] + [coded] * pieces,
        compiler_params=pltpu.CompilerParams(vmem_limit_bytes=8 << 20),
    )(over, own, *parts)


def choose_kernel(near_ref, first_ref, second_ref, out_ref):
    near = near_ref[0] > 0
    both = first_ref.shape[0] - META
    out_ref[:both, :] = jnp.where(near, second_ref[:both, :].astype(I32), first_ref[:both, :].astype(I32)).astype(I16)
    first, second = flags(first_ref), flags(second_ref)
    row = lax.broadcasted_iota(I32, (META, TILE), 0)
    out_ref[both:, :] = jnp.where((row >= RT) | near, second, first).astype(I16)


def choose(near, first, second):
    return pl.pallas_call(
        choose_kernel,
        in_specs=[SMEM] + [VMEM] * 2,
        out_specs=VMEM,
        out_shape=jax.ShapeDtypeStruct(first.shape, I16),
        compiler_params=pltpu.CompilerParams(vmem_limit_bytes=8 << 20),
    )(near, first, second)


def last_kernel(near_ref, first_ref, second_a, second_b, sent_ref, got_a, got_b, out_ref, over_ref):
    near = near_ref[0] > 0
    half = RT // 2
    for n, (second_ref, got_ref) in enumerate(((second_a, got_a), (second_b, got_b))):
        scale = scales(got_ref)
        for i in range(half):
            t = n * half + i
            mine = jnp.where(near, first_ref[t], second_ref[i])
            out_ref[:, t * TILE : (t + 1) * TILE] = (mine + decode(got_ref, scale, i)).astype(BF16)
    over_ref[0] = jnp.max(jnp.maximum(flags(sent_ref), flags(got_b))[RT:, :])


def last(near, first, seconds, sent, got):
    return pl.pallas_call(
        last_kernel,
        in_specs=[SMEM] + [VMEM] * 6,
        out_specs=[VMEM, SMEM],
        out_shape=[jax.ShapeDtypeStruct((TILE, RT * TILE), BF16), jax.ShapeDtypeStruct((1,), I32)],
        compiler_params=pltpu.CompilerParams(vmem_limit_bytes=8 << 20),
    )(near, first, *seconds, sent, *got)


def plain(amplitudes, integrals, amp_mask, int_mask):
    kept = (
        amplitudes.reshape(OWN, TILES, TILE) * amp_mask.astype(BF16)[:, :, None]
    ).reshape(OWN, TILES * TILE)
    copies = jnp.broadcast_to(kept, (32,) + kept.shape)
    every = lax.all_to_all(copies, ("xh", "z", "core"), 0, 0).reshape(32 * OWN, TILES * TILE)
    ints = (
        integrals.reshape(RT, TILE, TILES, TILE) * int_mask.astype(BF16)[:, None, :, None]
    ).reshape(integrals.shape)
    value = lax.dot_general(every, ints, (((1,), (1,)), ((), ())), preferred_element_type=F32)
    parts = lax.all_to_all(value.reshape(8, TILE, RT * TILE), ("xl", "y"), 0, 0)
    return jnp.sum(parts, axis=0).astype(BF16)


RING = [(2 * z, 2 * ((z + 1) % 8)) for z in range(8)] + [(2 * z + 1, 2 * ((z + 7) % 8) + 1) for z in range(8)]

SHIFT = (0, 0, -1, -1, -2, -2, 1, 1, 2, 2, -3, -3, 4, 3, 3, 4)
OTHER = (0, 1, 0, 1, 0, 1, 1, 0, 1, 0, 0, 1, 0, 1, 0, 1)


def local(amplitudes, integrals, amp_mask, int_mask):
    z, core, y = (lax.axis_index(name).astype(I32) for name in ("z", "core", "y"))
    near = lax.axis_index("xl") == lax.axis_index("xh")
    up = 1 - 2 * core

    far = (z + up * jnp.asarray(SHIFT, I32)) & 7
    rows = (((far >> 1) - y) & 3) * 4 + (far & 1) * 2 + (core ^ jnp.asarray(OTHER, I32))

    own = pack(amplitudes, amp_mask)

    def with_sibling(message):
        return jnp.concatenate([message, swap(message, "core")], axis=0)

    def hop(block):
        return lax.ppermute(block, ("z", "core"), RING)

    pair = with_sibling(own)
    first, far_pair = lax.optimization_barrier((hop(pair), with_sibling(swap(own, "xh"))))
    blocks = [[pair, first], [far_pair]]
    for chain in blocks:
        while len(chain) < 4:
            chain.append(hop(chain[-1]))
        chain.append(hop(chain[-1][:1]))
    two = [jnp.concatenate(chain[1:3], axis=0) for chain in blocks]
    rest = jnp.concatenate(blocks[0][3:], axis=0)

    def spread(parts):
        return [lax.ppermute(part, "y", [(i, (i + d + 1) % 4) for i in range(4)]) for d, part in enumerate(parts)]

    held = [blocks[0][0], two[0], swap(two[0], "core"), rest, swap(rest, "core")]
    own_part, *parts, over, kept_ints = first_chunk(rows, int_mask, integrals, held)
    over, late = lax.optimization_barrier((over, blocks[1][4]))
    rest = jnp.concatenate([blocks[1][3], late], axis=0)
    held = [blocks[1][0], two[1], swap(two[1], "core"), rest, swap(rest, "core")]
    first_sum, *first_coded = add(over, own_part, spread(parts), 2)

    near = near.astype(I32).reshape(1)
    seconds, got = [], []
    own_part, *parts, over, amps = second_chunk(rows, over, kept_ints, held)
    for half in range(2):
        if half == 1:
            own_part, *parts = second_half(over, kept_ints, amps)
        total, coded = add(over, own_part, spread(parts), 1)
        sent = choose(near, first_coded[half], coded)
        seconds.append(total)
        got.append(swap(sent, "xl"))
    out, over = last(near, first_sum, seconds, sent, got)
    return lax.cond(
        over[0] > 0,
        lambda out: plain(amplitudes, integrals, amp_mask, int_mask),
        lambda out: out,
        out,
    )


def solution(mesh):
    fine = Mesh(mesh.devices.reshape(2, 8, 2, 2, 4), ("xh", "z", "core", "xl", "y"))
    blk, col = ("xh", "z", "core"), ("xl", "y")
    return jax.shard_map(
        local, mesh=fine, in_specs=(P(blk, col),) * 4, out_specs=P(col, blk), check_vma=False
    )
```
